128 devices in a mesh: dp: 16 (over x, y), neg: 8 (over z, core).
Axes of the slice: x: 4, y: 4, z: 4, core: 2. Of those that a mesh axis runs over, the one named last changes fastest.
Arguments:
- queries: bfloat16 [8192, 4096], P('dp'), may hold values from -144 to 144, as said below
- passages: bfloat16 [32768, 4096], P(('dp', 'neg')), may hold values from -6 to 6
- list_owner: int32 [8, 2048, 1], P('neg', 'dp'), may hold values from 0 to 127; in each aligned block of 128 rows (0 to 127, 128 to 255, ..., all dimensions but the last counted through in order) at most 2 rows name the same one
- list_row: int32 [8, 2048], P('neg', 'dp'), may hold values from 0 to 255
- positive: int32 [8192], P('dp'), may hold values from 0 to 16383
- row_weight: float32 [8192], P('dp'), may hold values from 8 to 32
Outputs:
- query_grad: bfloat16 [8192, 4096], P('dp', 'neg')
- passage_grad: float32 [32768, 4096], P(('dp', 'neg'))
The draws below stay inside these ranges and needn't reach their ends.
Inputs may be any that keep to these rules, and one draw needn't show every extreme that they name: `queries`: queries are embedding activations. `list_owner`: among the 128 entries of one device no owner appears more than 2 times, and in every draw some device names some owner exactly 2 times.
All inputs are finite; a program needn't handle non-finite values.
Results may differ from the reference program's by a relative error of at most 0.015.
Values may be sent and summed in bfloat16 or wider, within the bound.
A program may use at most 192 MiB of HBM per device.

```python
import math
import jax
import jax.numpy as jnp
import numpy as np
from jax import lax

D = 4096
Q_DEV = 512
LIST_DEV = 128
PASS_DEV = 256
CAP = 2
QUERIES = 8192
PASSAGES = 32768
BLOCK = 2048
COLS = 16384
N_DP = 16
N_NEG = 8
DEVICES = 128


def draw_queries(key, part):
    key = jax.random.fold_in(key, 11)
    base = jnp.clip(jax.random.normal(key, (QUERIES, D), jnp.float32), -6.0, 6.0)
    return base.astype(jnp.bfloat16)


def place_ends(result, rng, smallest, top_value):
    longest = result.shape.index(max(result.shape))
    spots = []
    for shift in (0, 1):
        where = [jax.random.randint(jax.random.fold_in(rng, axis), (), 0, length) for axis, length in enumerate(result.shape)]
        where[longest] = (where[longest] + shift) % result.shape[longest]
        spots.append(tuple(where))
    return result.at[spots[0]].set(smallest).at[spots[1]].set(top_value)


def shard_levels(key, extent, split, smallest, top_value):
    def one(position, blocks):
        heights = jax.random.uniform(jax.random.fold_in(jax.random.fold_in(key, 6), position), (blocks,), jnp.float32, smallest / len(split), top_value / len(split))
        return jnp.repeat(jnp.exp(heights), extent[position] // blocks).reshape((-1,) + (1,) * (len(extent) - position - 1))

    gain = one(*split[0])
    for cut in split[1:]:
        gain = gain * one(*cut)
    return gain


def rank_table(count, slope):
    loads = [(1 << 20) // math.isqrt(grade ** slope) + 1 for grade in range(1, count + 1)]
    width = 1 + sum(loads) // (1 << 30)
    return np.cumsum(np.array([max(1, weight // width) for weight in loads]))


def skewed_ids(rng, dims, number_of, skew):
    table = rank_table(number_of, skew)
    ticket = jax.random.randint(jax.random.fold_in(rng, 1), dims, 0, int(table[number_of - 1]))
    grade = jnp.searchsorted(jnp.asarray(table, jnp.int32), ticket, side="right")
    return jax.random.permutation(jax.random.fold_in(rng, 2), number_of)[grade].astype(jnp.int32)


def deal_out(rng, own, number, rows, count, top, limit, slope):
    sequence = jax.random.permutation(rng, count)
    packed, ordinary = shares(count, rows * top, limit, slope, True), shares(count, rows * top, limit, slope, False)
    places = jnp.arange(count)

    def named(lengths, turn):
        used = int((lengths > 0).sum())
        fixed = max(1, used // 4)
        passed = fixed + (places - fixed + turn * (used - fixed)) % max(1, count - fixed)
        return jnp.zeros((count,), jnp.int32).at[sequence[jnp.where(places < fixed, places, passed)]].set(jnp.asarray(lengths, jnp.int32))

    lengths = jnp.where(number % 4 == 0, named(packed, number // 4), named(ordinary, number - number // 4 - 1))
    mixed = jax.random.permutation(jax.random.fold_in(own, 3), count)
    source_of, sink = mixed[0:count // 2 * 2:2], mixed[1:count // 2 * 2:2]
    room = jnp.minimum(lengths[source_of] - 1, limit - lengths[sink]) // 2
    room = jnp.where((source_of == sequence[0]) | (sink == sequence[0]) | (lengths[sink] == 0), 0, jnp.maximum(room, 0))
    passed = jax.random.randint(jax.random.fold_in(own, 4), (count // 2,), 0, 1 << 20) % (room + 1)
    lengths = lengths.at[source_of].add(-passed).at[sink].add(passed)
    members = jnp.searchsorted(jnp.cumsum(lengths), jnp.arange(rows * top), side="right").astype(jnp.int32)
    grid = members.reshape(top, rows).T
    grid = grid[jax.random.permutation(jax.random.fold_in(own, 1), rows)]
    turn = jax.random.randint(jax.random.fold_in(own, 2), (rows, 1), 0, top)
    return jnp.take_along_axis(grid, (jnp.arange(top)[None, :] + turn) % top, axis=1)


def shares(count, total, most, skew, full):
    loads = [(1 << 20) // math.isqrt(grade ** skew) + 1 for grade in range(1, count + 1)]
    largest = most if full else min(most, max(-(-total // count), total * loads[0] // sum(loads)))
    least = 1 if total - largest >= count - 1 else 0
    counts, spare = [largest] + [least] * (count - 1), total - largest - least * (count - 1)
    while spare > 0:
        movable = [i for i in range(1, count) if counts[i] < largest] or [i for i in range(1, count) if counts[i] < most]
        whole, left = sum([loads[i] for i in movable]), spare
        for i in movable:
            more = min(most - counts[i], max(1, left * loads[i] // whole), spare)
            counts[i] = counts[i] + more
            spare = spare - more
    return np.array(counts)


def gaussian(stream_key, shape, deviation, limit, cuts=(), kind=jnp.bfloat16):
    result = jax.random.normal(stream_key, shape, jnp.float32) * deviation
    if len(cuts) > 0:
        result = shard_levels(stream_key, shape, cuts, -0.22, 0.18) * result
    return jnp.clip(result, min=-limit, max=limit).astype(kind)


def setup_inputs(seed: int = 0) -> dict:
    key_of = jax.random.split(jax.random.key(seed), 7)
    queries = draw_queries(jax.random.fold_in(key_of[6], 71), 0)
    passages = gaussian(key_of[1], (PASSAGES, D), 1.0, 6.0, ((0, 128),))
    list_owner_keys = jax.random.split(jax.random.fold_in(key_of[2], 1), N_NEG * BLOCK // LIST_DEV)
    list_owner_turns = jax.random.permutation(jax.random.fold_in(key_of[2], 3), N_NEG * BLOCK // LIST_DEV)
    list_owner = jax.vmap(lambda own, number: deal_out(jax.random.fold_in(key_of[2], 2), own, number, LIST_DEV, DEVICES, 1, CAP, 2))(list_owner_keys, list_owner_turns).reshape((N_NEG, BLOCK, 1))
    list_row = place_ends(skewed_ids(key_of[3], (N_NEG, BLOCK), PASS_DEV, 2), jax.random.fold_in(key_of[3], 3), 0, PASS_DEV - 1).astype(jnp.int32)
    positive = place_ends(jax.random.randint(key_of[4], (QUERIES,), 0, COLS), jax.random.fold_in(key_of[4], 1), 0, COLS - 1).astype(jnp.int32)
    row_weight = jnp.clip(jnp.exp(math.log(32.0) - 1.3862944 * jax.random.uniform(key_of[5], (QUERIES,), jnp.float32) ** shard_levels(key_of[5], (QUERIES,), ((0, 16),), -0.2, 0.2)), 8.0, 32.0)
    return dict(queries=queries, passages=passages, list_owner=list_owner, list_row=list_row, positive=positive, row_weight=row_weight)


def reference(queries, passages, list_owner, list_row, positive, row_weight):
    passage_ids = (list_owner[..., 0] * PASS_DEV + list_row).reshape(-1).astype(jnp.int32)
    columns = passages[passage_ids]
    logit_scale = 3.0 / math.sqrt(D)
    query_blocks = queries.reshape(N_DP, Q_DEV, D)
    pos_blocks = positive.reshape(N_DP, Q_DEV)
    weight_blocks = row_weight.reshape(N_DP, Q_DEV)
    col_index = jnp.arange(COLS, dtype=jnp.int32)

    def per_shard(carry, inputs):
        query_rows, pos_rows, weight_rows = inputs
        logits = jnp.dot(query_rows, columns.T, preferred_element_type=jnp.float32) * logit_scale
        row_max = lax.optimization_barrier(jnp.max(logits, axis=1, keepdims=True))
        expo = jnp.exp(logits - row_max)
        row_total = lax.optimization_barrier(jnp.sum(expo, axis=1, keepdims=True))
        target = (col_index[None, :] == pos_rows[:, None]).astype(jnp.float32)
        logit_grad = (weight_rows[:, None] * logit_scale * (expo / row_total - target)).astype(jnp.bfloat16)
        query_sum = jnp.zeros((Q_DEV, D), jnp.float32)
        for block_idx in range(N_NEG):
            lower = block_idx * BLOCK
            partial_value = jnp.dot(logit_grad[:, lower:lower + BLOCK], columns[lower:lower + BLOCK], preferred_element_type=jnp.float32)
            query_sum = query_sum + lax.optimization_barrier(partial_value.astype(jnp.bfloat16)).astype(jnp.float32)
        term = lax.dot_general(logit_grad, query_rows, (((0,), (0,)), ((), ())), preferred_element_type=jnp.float32)
        term = lax.optimization_barrier(term.astype(jnp.bfloat16)).astype(jnp.float32)
        return (carry + term, query_sum.astype(jnp.bfloat16))
    column_grad, query_grad = lax.scan(per_shard, jnp.zeros((COLS, D), jnp.float32), (query_blocks, pos_blocks, weight_blocks))
    passage_grad = jnp.zeros((PASSAGES, D), jnp.float32).at[passage_ids].add(column_grad)
    return (query_grad.reshape(QUERIES, D), passage_grad)
```

```python
import math

import jax
import jax.numpy as jnp
from jax import lax
from jax.experimental import pallas as pl
from jax.experimental.pallas import tpu as pltpu
from jax.sharding import PartitionSpec as P

MESH = pl.DeviceIdType.MESH
BF16 = jnp.bfloat16
F32 = jnp.float32
RING = 4
N_NEG = 8
LOW = -3.0e38

NN = (((1,), (0,)), ((), ()))
NT = (((1,), (1,)), ((), ()))
TN = (((0,), (0,)), ((), ()))


def dot(a, b, dims):
    return lax.dot_general(a, b, dims, preferred_element_type=F32)


class Sems:
    def __init__(self, ref):
        self.ref = ref
        self.used = 0

    def new(self):
        self.used += 1
        return self.ref.at[self.used - 1]


class RingScatter:
    def __init__(self, sems, right, left, view, first, second):
        self.view, self.first, self.second = view, first, second
        self.up, self.down = right, left
        self.sem = [(sems.new(), sems.new()) for _ in range(4)]
        self.copies = []

    def send(self, src, dst, index, to):
        copy = pltpu.make_async_remote_copy(
            src, dst, self.sem[index][0], self.sem[index][1], device_id=to, device_id_type=MESH
        )
        copy.start()
        self.copies.append(copy)
        return copy

    def start(self):
        self.a = self.send(self.view(2, 0), self.first.at[0], 0, self.up)
        self.b = self.send(self.view(2, 1), self.first.at[1], 1, self.down)

    def middle(self):
        self.a.wait_recv()
        self.b.wait_recv()
        part = self.view(1, 0)
        part[...] = (part[...].astype(F32) + self.first[0].astype(F32)).astype(BF16)
        self.c = self.send(self.view(1, None), self.second(0), 2, self.up)
        part = self.view(3, 1)
        part[...] = (part[...].astype(F32) + self.first[1].astype(F32)).astype(BF16)
        self.d = self.send(self.view(3, None), self.second(1), 3, self.down)

    def finish(self, dst):
        self.c.wait_recv()
        self.d.wait_recv()
        own = self.view(0, None)[...].astype(F32)
        dst[...] = (own + self.second(0)[...].astype(F32) + self.second(1)[...].astype(F32)).astype(BF16)

    def drain(self):
        for copy in self.copies:
            copy.wait_send()


def kernel(
    q_in, p_in, ids_in, pos_in, w_in,
    q_out, p_out, land,
    qv, pv, px, ev, gv, gx, pg, pg_first,
    ay1, az1, az2, bz1, by1, by2, q_res,
    ids, table, count, wp, m_b, s_b, st_own, st_in, st_mid, st_y, factor,
    sem_ref,
):
    dp, neg = lax.axis_index("dp"), lax.axis_index("neg")
    x, y = dp // RING, dp % RING
    z, core = neg // 2, neg % 2
    block, width = q_in.shape
    owned = p_in.shape[0]
    strip = width // N_NEG
    scale = 3.0 / math.sqrt(width)
    sems = Sems(sem_ref)

    def device(xx, yy, zz, cc):
        return ((xx % RING) * RING + yy % RING, (zz % RING) * 2 + cc)

    x_peer = [None] + [device(x + k, y, z, core) for k in (1, 2, 3)]
    y_peer = [None] + [device(x, y + k, z, core) for k in (1, 2, 3)]
    z_up, z_down = device(x, y, z + 1, core), device(x, y, z + 3, core)
    other = device(x, y, z, 1 - core)
    n_peer = [None] + [(dp, (neg + k) % N_NEG) for k in range(1, N_NEG)]

    barrier = pltpu.get_barrier_semaphore()
    greeted = x_peer[1:] + y_peer[1:] + n_peer[1:]
    for peer in greeted:
        pl.semaphore_signal(barrier, inc=1, device_id=peer, device_id_type=MESH)
    pl.semaphore_wait(barrier, len(greeted))

    sent = []

    def send(src, dst, to):
        copy = pltpu.make_async_remote_copy(
            src, dst, sems.new(), sems.new(), device_id=to, device_id_type=MESH
        )
        copy.start()
        sent.append(copy)
        return copy

    half = owned // 2
    lo, hi = pl.ds(0, half), pl.ds(half, half)
    p_right = [send(p_in.at[lo], pv.at[3, lo], x_peer[1])]
    p_left = [send(p_in.at[hi], pv.at[1, hi], x_peer[3])]
    piece = block // 8

    def rows(zz, cc, sub):
        return pl.ds(pl.multiple_of(zz * (4 * piece) + cc * (2 * piece) + sub * piece, piece), piece)

    zp = z % 2
    q_right = [send(q_in.at[rows(zp, core, 0)], qv.at[3, rows(zp, core, 0)], y_peer[1])]
    q_left = [send(q_in.at[rows(zp, core, 1)], qv.at[1, rows(zp, core, 1)], y_peer[3])]

    own_q = pltpu.make_async_copy(q_in, qv.at[0], sems.new())
    own_p = pltpu.make_async_copy(p_in, pv.at[0], sems.new())
    own_p.start()
    own_q.start()

    ids[dp, neg] = ids_in[0]
    copies = [send(ids.at[dp, neg], ids.at[dp, neg], n_peer[k]) for k in range(1, N_NEG)]
    p_right.append(send(p_in.at[hi], pv.at[3, hi], x_peer[1]))
    p_left.append(send(p_in.at[lo], pv.at[1, lo], x_peer[3]))
    q_right.append(send(q_in.at[rows(zp, core, 1)], qv.at[3, rows(zp, core, 1)], y_peer[1]))
    q_left.append(send(q_in.at[rows(zp, core, 0)], qv.at[1, rows(zp, core, 0)], y_peer[3]))
    for copy in copies:
        copy.wait_recv()
    copies = [send(ids.at[dp], ids.at[dp], y_peer[k]) for k in (1, 2, 3)]
    for copy in copies:
        copy.wait_recv()
    line = ids.at[pl.ds(x * RING, RING)]
    copies = [send(line, line, x_peer[k]) for k in (1, 2, 3)]
    for copy in copies:
        copy.wait_recv()

    lanes = ids.shape[-1]
    first_id = (dp * N_NEG + neg) * owned
    name = lax.broadcasted_iota(jnp.int32, (owned, lanes), 0) + first_id

    def tally(i, total):
        for j in range(N_NEG):
            total = total + jnp.where(name == ids[i, j], 1.0, 0.0)
        return total

    total = lax.fori_loop(0, RING * RING, tally, jnp.zeros((owned, lanes), F32))
    count[0] = dot(total.astype(BF16), jnp.ones((lanes, lanes), BF16), NN)
    counts = [send(count.at[0], count.at[4 - k], x_peer[k]) for k in (1, 2, 3)]

    for i in range(RING * RING):
        for j in range(N_NEG):
            table[pl.ds(i * N_NEG + j, 1), :] = ids[i, j]
    pos = pos_in[...]
    entry = jnp.bitwise_and(pos, lanes - 1)
    listing = jnp.bitwise_and(pos // lanes, RING * RING - 1) * N_NEG + pos // (lanes * RING * RING)
    side = lax.broadcasted_iota(jnp.int32, (lanes, block), 0)
    chosen = jnp.where(side == listing, 1.0, 0.0).astype(BF16)
    high = (table[...] // 256).astype(F32).astype(BF16)
    low = jnp.bitwise_and(table[...], 255).astype(F32).astype(BF16)
    found = dot(high, chosen, TN) * 256.0 + dot(low, chosen, TN)
    wp[0, 0:1, :] = w_in[...] * scale
    wp[0, 1:2, :] = jnp.sum(jnp.where(side == entry, found, 0.0), axis=0, keepdims=True)
    targets = [send(wp.at[0], wp.at[4 - k], y_peer[k]) for k in (1, 2, 3)]

    def logits(b, r):
        listed = count[b]
        listed = jnp.concatenate([listed] * (block // lanes), axis=1)
        value = dot(pv[b], qv[r], NT) * scale
        value = jnp.where(listed > 0.0, value, LOW)
        top = jnp.max(value, axis=0, keepdims=True)
        expo = jnp.exp(value - top) * listed
        place = pl.ds(pl.multiple_of(r * block, block), block)
        ev[b, :, place] = expo
        m_b[b, :, place] = top
        s_b[b, :, place] = jnp.sum(expo, axis=0, keepdims=True)

    own_p.wait()
    own_q.wait()
    logits(0, 0)

    from_z, from_core = {}, {}

    def pass_on(r, sub):
        view = qv.at[r, rows(zp, core, sub)]
        from_z[r, sub] = send(view, view, z_up if sub == 0 else z_down)
        from_core[r, 0, sub] = send(view, view, other)

    def pass_over(r, sub):
        from_z[r, sub].wait_recv()
        view = qv.at[r, rows(1 - zp, core, sub)]
        from_core[r, 1, sub] = send(view, view, other)

    def have(r):
        for key in from_core:
            if key[0] == r:
                from_core[key].wait_recv()

    def to_core(b):
        for k in range(RING):
            col = pl.ds(pl.multiple_of((((z + k) % RING) * 2 + 1 - core) * strip, strip), strip)
            crossed.append(send(pv.at[b, :, col], px.at[k, b], other))

    crossed = []
    to_core(0)
    q_right[0].wait_recv()
    q_far0 = send(qv.at[3, rows(zp, core, 0)], qv.at[2, rows(zp, core, 0)], y_peer[1])
    pass_on(3, 0)
    q_left[0].wait_recv()
    q_far1 = send(qv.at[1, rows(zp, core, 1)], qv.at[2, rows(zp, core, 1)], y_peer[3])
    pass_on(1, 1)
    p_right[0].wait_recv()
    p_far0 = send(pv.at[3, lo], pv.at[2, lo], x_peer[1])
    p_left[0].wait_recv()
    p_far1 = send(pv.at[1, hi], pv.at[2, hi], x_peer[3])
    q_right[1].wait_recv()
    pass_on(3, 1)
    q_left[1].wait_recv()
    pass_on(1, 0)
    pass_over(3, 0)
    pass_over(1, 1)
    q_far0.wait_recv()
    pass_on(2, 0)
    q_far1.wait_recv()
    pass_on(2, 1)
    pass_over(3, 1)
    pass_over(1, 0)
    have(1)
    have(3)
    pl.loop(0, 2)(lambda j: logits(0, 1 + 2 * j))
    for copy in counts + targets:
        copy.wait_recv()
    p_right[1].wait_recv()
    p_left[1].wait_recv()
    to_core(1)
    to_core(3)

    @pl.loop(0, 6)
    def _(i):
        j = i % 3
        logits(1 + 2 * (i // 3), j + j // 2)

    pass_over(2, 0)
    pass_over(2, 1)
    have(2)
    pl.loop(0, 3)(lambda i: logits(i + i // 2, 2))
    p_far0.wait_recv()
    p_far1.wait_recv()
    pl.loop(0, 4)(lambda r: logits(2, r))
    to_core(2)

    top = jnp.maximum(jnp.maximum(m_b[0], m_b[1]), jnp.maximum(m_b[2], m_b[3]))
    st_own[0:1, :] = top
    st_own[1:2, :] = sum(s_b[b] * jnp.exp(m_b[b] - top) for b in range(RING))
    copies = [send(st_own, st_in.at[k], n_peer[k]) for k in range(1, N_NEG)]
    for copy in copies:
        copy.wait_recv()
    for k in range(1, N_NEG):
        top = jnp.maximum(top, st_in[k, 0:1, :])
    mass = st_own[1:2, :] * jnp.exp(st_own[0:1, :] - top)
    for k in range(1, N_NEG):
        mass = mass + st_in[k, 1:2, :] * jnp.exp(st_in[k, 0:1, :] - top)
    st_mid[0:1, :] = top
    st_mid[1:2, :] = mass
    copies = [send(st_mid, st_y.at[k], y_peer[k]) for k in (1, 2, 3)]
    for copy in copies:
        copy.wait_recv()
    for r in range(RING):
        mine = pl.ds(r * block, block)
        theirs = [(k, pl.ds(((r + k) % RING) * block, block)) for k in (1, 2, 3)]
        top = st_mid[0:1, mine]
        for k, place in theirs:
            top = jnp.maximum(top, st_y[k, 0:1, place])
        mass = st_mid[1:2, mine] * jnp.exp(st_mid[0:1, mine] - top)
        for k, place in theirs:
            mass = mass + st_y[k, 1:2, place] * jnp.exp(st_y[k, 0:1, place] - top)
        weight = wp[r, 0:1, :] / mass
        for b in range(RING):
            factor[b, :, mine] = jnp.exp(m_b[b, :, mine] - top) * weight

    def gradient(b):
        base = ((((x + b) % RING) * RING + y) * N_NEG + neg) * owned
        label = (lax.broadcasted_iota(jnp.int32, (owned, block), 0) + base).astype(F32)
        for r in range(RING):
            place = pl.ds(r * block, block)
            hit = jnp.where(label == wp[r, 1:2, :], wp[r, 0:1, :], 0.0)
            gv[b, :, place] = (ev[b, :, place] * factor[b, :, place] - hit).astype(BF16)

    wide = width // 4

    def passage_part(b, n):
        col = pl.ds(pl.multiple_of(n * wide, wide), wide)
        return dot(gv[b], qv[:, :, col].reshape(RING * block, wide), NN)

    far = {}
    gradient(2)
    for n in (0, 2, 1, 3):
        col = pl.ds(n * wide, wide)
        pg[1, :, col] = passage_part(2, n).astype(BF16)
        far[n] = send(pg.at[1, :, col], pg_first.at[n], x_peer[1] if n < 2 else x_peer[3])
    grads = [send(gv.at[2], gx.at[2], other)]
    for b in (1, 3, 0):
        gradient(b)
        grads.append(send(gv.at[b], gx.at[b], other))

    @pl.loop(0, 8)
    def _(i):
        b = 1 + 2 * (i // 4)
        col = pl.ds(pl.multiple_of((i % 4) * wide, wide), wide)
        pg[b - 1, :, col] = passage_part(b, i % 4).astype(BF16)

    @pl.loop(0, 4)
    def _(n):
        col = pl.ds(pl.multiple_of((n % 2) * wide, wide), wide)
        ev[n // 2, :, col] = passage_part(0, n)

    near = {}
    before = len(sent)
    for n in (2, 3, 0, 1):
        col = pl.ds(n * wide, wide)
        b = 1 if n >= 2 else 3
        near[b, n] = send(pg.at[b - 1, :, col], land.at[0 if b == 1 else 1, n], x_peer[b])
    for n in (0, 1, 2, 3):
        col = pl.ds(n * wide, wide)
        b = 1 if n < 2 else 3
        far[n].wait_recv()
        pg[b - 1, :, col] = (pg[b - 1, :, col].astype(F32) + pg_first[n].astype(F32)).astype(BF16)
        near[b, n] = send(pg.at[b - 1, :, col], land.at[0 if b == 1 else 1, n], x_peer[b])

    for copy in sent[:before]:
        copy.wait_send()
    for copy in grads + crossed:
        copy.wait_recv()

    def query_part(r):
        place = pl.ds(pl.multiple_of(r * block, block), block)

        @pl.loop(0, RING)
        def _(k):
            col = pl.ds(pl.multiple_of((((z + k) % RING) * 2 + core) * strip, strip), strip)
            mine = dot(
                gv[:, :, place].reshape(RING * owned, block),
                pv[:, :, col].reshape(RING * owned, strip),
                TN,
            )
            theirs = dot(
                gx[:, :, place].reshape(RING * owned, block),
                px[k].reshape(RING * owned, strip),
                TN,
            )
            out = pl.ds(pl.multiple_of(k * strip, strip), strip)
            qv[r, :, out] = (mine + theirs).astype(BF16)

    mid = block // 2
    quarter = mid // 2

    def upper(rel, part):
        at = pl.ds(0, mid) if part is None else pl.ds(part * quarter, quarter)
        return qv.at[rel, at, pl.ds(0, RING * strip)]

    def lower(rel, part):
        at = pl.ds(mid, mid) if part is None else pl.ds(mid + part * quarter, quarter)
        return qv.at[rel, at, pl.ds(0, strip)]

    def across(r, start):
        def view(rel, part):
            at = pl.ds(start, mid) if part is None else pl.ds(start + part * quarter, quarter)
            return qv.at[r, at, pl.ds(rel * strip, strip)]

        return view

    def spare_upper(way):
        return qv.at[way, pl.ds(0, mid), pl.ds(RING * strip, RING * strip)]

    def spare_lower(r):
        return lambda way: qv.at[r, pl.ds(mid, mid), pl.ds((RING + way) * strip, strip)]

    def slots(ref):
        return lambda way: ref.at[way]

    a_y = RingScatter(sems, y_peer[1], y_peer[3], upper, ay1, spare_upper)
    a_z = RingScatter(sems, z_up, z_down, across(0, 0), az1, slots(az2))
    b_y = RingScatter(sems, y_peer[1], y_peer[3], lower, by1, slots(by2))
    b_z = {
        r: RingScatter(sems, z_up, z_down, across(r, mid), bz1.at[r], spare_lower(r)) for r in range(RING)
    }

    query_part(2)
    a_y.start()
    b_z[2].start()
    query_part(1)
    b_z[1].start()
    query_part(3)
    b_z[3].start()
    b_z[2].middle()
    a_y.middle()
    query_part(0)
    b_z[0].start()
    b_z[1].middle()
    b_z[3].middle()
    b_z[2].finish(lower(2, None))
    b_y.start()
    b_z[0].middle()
    b_z[1].finish(lower(1, None))
    b_z[3].finish(lower(3, None))
    b_y.middle()
    b_z[0].finish(lower(0, None))
    a_y.finish(upper(0, None))
    a_z.start()
    a_z.middle()
    b_y.finish(q_res.at[pl.ds(mid, mid)])
    a_z.finish(q_res.at[pl.ds(0, mid)])
    q_copy = pltpu.make_async_copy(q_res, q_out, sems.new())
    q_copy.start()

    loads, stores = {}, []
    for n in (0, 3, 1, 2):
        col = pl.ds(n * wide, wide)
        for b in (1, 3):
            near[b, n].wait()
            loads[b, n] = pltpu.make_async_copy(land.at[0 if b == 1 else 1, n], pg.at[b - 1, :, col], sems.new())
            loads[b, n].start()
    for n in (0, 3, 1, 2):
        col = pl.ds(n * wide, wide)
        inner = pl.ds((n % 2) * wide, wide)
        loads[1, n].wait()
        loads[3, n].wait()
        ev[n // 2, :, inner] = ev[n // 2, :, inner] + pg[0, :, col].astype(F32) + pg[2, :, col].astype(F32)
        store = pltpu.make_async_copy(ev.at[n // 2, :, inner], p_out.at[:, col], sems.new())
        store.start()
        stores.append(store)
    for ring in [a_y, a_z, b_y] + list(b_z.values()):
        ring.drain()
    q_copy.wait()
    for store in stores:
        store.wait()


def body(queries, passages, list_owner, list_row, positive, row_weight):
    block, width = queries.shape
    owned = passages.shape[0]
    lanes = list_row.shape[1]
    strip = width // N_NEG
    mid = block // 2
    ids = (list_owner.reshape(1, 1, lanes) * owned + list_row.reshape(1, 1, lanes)).astype(jnp.int32)
    any_space = pl.BlockSpec(memory_space=pl.ANY)
    vmem = pl.BlockSpec(memory_space=pltpu.VMEM)
    wide = width // 4
    scratch = [
        pltpu.VMEM((RING, block, width), BF16),
        pltpu.VMEM((RING, owned, width), BF16),
        pltpu.VMEM((RING, RING, owned, strip), BF16),
        pltpu.VMEM((RING, owned, RING * block), F32),
        pltpu.VMEM((RING, owned, RING * block), BF16),
        pltpu.VMEM((RING, owned, RING * block), BF16),
        pltpu.VMEM((3, owned, width), BF16),
        pltpu.VMEM((4, owned, wide), BF16),
        pltpu.VMEM((2, mid // 2, RING * strip), BF16),
        pltpu.VMEM((2, mid // 2, strip), BF16),
        pltpu.VMEM((2, mid, strip), BF16),
        pltpu.VMEM((RING, 2, mid // 2, strip), BF16),
        pltpu.VMEM((2, mid // 2, strip), BF16),
        pltpu.VMEM((2, mid, strip), BF16),
        pltpu.VMEM((block, strip), BF16),
        pltpu.VMEM((RING * RING, N_NEG, 1, lanes), jnp.int32),
        pltpu.VMEM((lanes, lanes), jnp.int32),
        pltpu.VMEM((RING, owned, lanes), F32),
        pltpu.VMEM((RING, 2, block), F32),
        pltpu.VMEM((RING, 1, RING * block), F32),
        pltpu.VMEM((RING, 1, RING * block), F32),
        pltpu.VMEM((2, RING * block), F32),
        pltpu.VMEM((N_NEG, 2, RING * block), F32),
        pltpu.VMEM((2, RING * block), F32),
        pltpu.VMEM((RING, 2, RING * block), F32),
        pltpu.VMEM((RING, 1, RING * block), F32),
        pltpu.SemaphoreType.DMA((256,)),
    ]
    flops = 6 * RING * block * RING * owned * width
    query_grad, passage_grad, _ = pl.pallas_call(
        kernel,
        out_shape=(
            jax.ShapeDtypeStruct((block, strip), BF16),
            jax.ShapeDtypeStruct((owned, width), F32),
            jax.ShapeDtypeStruct((2, 4, owned, wide), BF16),
        ),
        in_specs=[any_space, any_space, vmem, vmem, vmem],
        out_specs=(any_space, any_space, any_space),
        scratch_shapes=scratch,
        compiler_params=pltpu.CompilerParams(
            collective_id=0, has_side_effects=True, vmem_limit_bytes=60 * 2**20
        ),
        cost_estimate=pl.CostEstimate(flops=flops, bytes_accessed=40 * 2**20, transcendentals=0),
        name="contrastive",
    )(queries, passages, ids, positive.reshape(1, block), row_weight.reshape(1, block))
    return query_grad, passage_grad


def solution(mesh):
    in_specs = (
        P("dp", None),
        P(("dp", "neg"), None),
        P("neg", "dp", None),
        P("neg", "dp"),
        P("dp"),
        P("dp"),
    )
    out_specs = (P("dp", "neg"), P(("dp", "neg"), None))
    return jax.shard_map(body, mesh=mesh, in_specs=in_specs, out_specs=out_specs, check_vma=False)
```

```python
import math

import jax
import jax.numpy as jnp
from jax import lax
from jax.experimental import pallas as pl
from jax.experimental.pallas import tpu as pltpu
from jax.sharding import PartitionSpec as P

MESH = pl.DeviceIdType.MESH
BF16 = jnp.bfloat16
F32 = jnp.float32
RING = 4
N_NEG = 8
SEMS = 320
LOW = -3.0e38
LOG2E = 1.0 / math.log(2.0)

NN = (((1,), (0,)), ((), ()))
NT = (((1,), (1,)), ((), ()))
TN = (((0,), (0,)), ((), ()))


def dot(a, b, dims):
    return lax.dot_general(a, b, dims, preferred_element_type=F32)


class Sems:
    def __init__(self, ref):
        self.ref = ref
        self.used = 0

    def new(self):
        self.used += 1
        assert self.used <= SEMS
        return self.ref.at[self.used - 1]


class Copy:
    def __init__(self, copy):
        self.copy, self.landed, self.left = copy, False, False
        copy.start()

    def wait_recv(self):
        if not self.landed:
            self.copy.wait_recv()
        self.landed = True

    def wait_send(self):
        if not self.left:
            self.copy.wait_send()
        self.left = True

    def wait(self):
        self.wait_recv()
        self.wait_send()


class RingScatter:
    def __init__(self, send, right, left, view, first, second):
        self.view, self.first, self.second = view, first, second
        self.up, self.down, self.send = right, left, send

    def start(self):
        self.a = self.send(self.view(2, 0), self.first.at[0], self.up)
        self.b = self.send(self.view(2, 1), self.first.at[1], self.down)

    def middle(self):
        self.a.wait_recv()
        self.b.wait_recv()
        part = self.view(1, 0)
        part[...] = (part[...].astype(F32) + self.first[0].astype(F32)).astype(BF16)
        self.c = self.send(self.view(1, None), self.second(0), self.up)
        part = self.view(3, 1)
        part[...] = (part[...].astype(F32) + self.first[1].astype(F32)).astype(BF16)
        self.d = self.send(self.view(3, None), self.second(1), self.down)

    def arrive(self):
        self.c.wait_recv()
        self.d.wait_recv()

    def finish(self):
        self.arrive()
        own = self.view(0, None)
        total = own[...].astype(F32) + self.second(0)[...].astype(F32) + self.second(1)[...].astype(F32)
        own[...] = total.astype(BF16)

    def drain(self):
        for copy in self.copies:
            copy.wait_send()


def kernel(
    q_in, p_in, owner_in, row_in, pos_in, w_in,
    q_own, q_land, p_own, p_land,
    qv, pv, px, ev, gv, gx, pg, pg_first, ay1, az1, bz1, by1,
    ids, table, count, wp, m_b, s_b, st_own, st_in, st_mid, st_y, factor,
    sem_ref,
):
    dp, neg = lax.axis_index("dp"), lax.axis_index("neg")
    x, y = dp // RING, dp % RING
    z, core = neg // 2, neg % 2
    block, width = q_in.shape
    owned = p_in.shape[0]
    strip = width // N_NEG
    scale = 3.0 / math.sqrt(width)
    sems = Sems(sem_ref)

    def device(xx, yy, zz, cc):
        return ((xx % RING) * RING + yy % RING, (zz % RING) * 2 + cc)

    x_peer = [None] + [device(x + k, y, z, core) for k in (1, 2, 3)]
    y_peer = [None] + [device(x, y + k, z, core) for k in (1, 2, 3)]
    z_up, z_down = device(x, y, z + 1, core), device(x, y, z + 3, core)
    other = device(x, y, z, 1 - core)
    n_peer = [None] + [(dp, (neg + k) % N_NEG) for k in range(1, N_NEG)]

    barrier = pltpu.get_barrier_semaphore()
    greeted = x_peer[1:] + y_peer[1:] + n_peer[1:]
    for peer in greeted:
        pl.semaphore_signal(barrier, inc=1, device_id=peer, device_id_type=MESH)
    pl.semaphore_wait(barrier, len(greeted))

    sent = []

    def send(src, dst, to):
        copy = pltpu.make_async_remote_copy(
            src, dst, sems.new(), sems.new(), device_id=to, device_id_type=MESH
        )
        sent.append(Copy(copy))
        return sent[-1]

    half = owned // 2
    lo, hi = pl.ds(0, half), pl.ds(half, half)
    piece = block // 8
    zp = z % 2

    def rows(zz, cc, sub):
        return pl.ds(pl.multiple_of(zz * (4 * piece) + cc * (2 * piece) + sub * piece, piece), piece)

    ids[neg, y, x] = owner_in[...] * owned + row_in[...]
    copies = [send(ids.at[neg, y, x], ids.at[neg, y, x], x_peer[k]) for k in (1, 2, 3)]
    p_right = [send(p_in.at[lo], pv.at[3, lo], x_peer[1])]
    p_left = [send(p_in.at[hi], pv.at[1, hi], x_peer[3])]
    own_q = pltpu.make_async_copy(q_in, qv.at[0], sems.new())
    own_p = pltpu.make_async_copy(p_in, pv.at[0], sems.new())
    own_p.start()
    own_q.start()
    for copy in copies:
        copy.wait_recv()
    copies = [send(ids.at[neg, y], ids.at[neg, y], y_peer[k]) for k in (1, 2, 3)]
    q_right = [send(q_in.at[rows(zp, core, 0)], qv.at[3, rows(zp, core, 0)], y_peer[1])]
    q_left = [send(q_in.at[rows(zp, core, 1)], qv.at[1, rows(zp, core, 1)], y_peer[3])]
    for copy in copies:
        copy.wait_recv()
    copies = [send(ids.at[neg], ids.at[neg], n_peer[k]) for k in range(1, N_NEG)]
    p_right.append(send(p_in.at[hi], pv.at[3, hi], x_peer[1]))
    p_left.append(send(p_in.at[lo], pv.at[1, lo], x_peer[3]))
    q_right.append(send(q_in.at[rows(zp, core, 1)], qv.at[3, rows(zp, core, 1)], y_peer[1]))
    q_left.append(send(q_in.at[rows(zp, core, 0)], qv.at[1, rows(zp, core, 0)], y_peer[3]))
    for copy in copies:
        copy.wait_recv()

    lanes = ids.shape[-1]

    def first_id(b):
        return ((((x + b) % RING) * RING + y) * N_NEG + neg) * owned

    def tally(b):
        name = lax.broadcasted_iota(jnp.int32, (owned, lanes), 0) + first_id(b)

        def more(i, total):
            for j in range(RING * RING):
                total = total + jnp.where(name == ids[i, j // RING, j % RING], 1.0, 0.0)
            return total

        total = lax.fori_loop(0, N_NEG, more, jnp.zeros((owned, lanes), F32))
        listed = dot(total.astype(BF16), jnp.ones((lanes, lanes), BF16), NN)
        count[b] = jnp.where(listed > 0.0, jnp.log(jnp.maximum(listed, 1.0)) * LOG2E, LOW)

    tally(0)

    for i in range(N_NEG):
        for j in range(RING * RING):
            table[pl.ds(i * RING * RING + j, 1), :] = ids[i, j // RING, j % RING]
    pos = pos_in[...]
    entry = jnp.bitwise_and(pos, lanes - 1)
    lister = pos // lanes
    listing = (
        (lister // (RING * RING)) * (RING * RING)
        + jnp.bitwise_and(lister, RING - 1) * RING
        + jnp.bitwise_and(lister // RING, RING - 1)
    )
    side = lax.broadcasted_iota(jnp.int32, (lanes, block), 0)
    chosen = jnp.where(side == listing, 1.0, 0.0).astype(BF16)
    high = (table[...] // 256).astype(F32).astype(BF16)
    low = jnp.bitwise_and(table[...], 255).astype(F32).astype(BF16)
    found = dot(high, chosen, TN) * 256.0 + dot(low, chosen, TN)
    wp[0, 0:1, :] = w_in[...] * scale
    wp[0, 1:2, :] = jnp.sum(jnp.where(side == entry, found, 0.0), axis=0, keepdims=True)
    targets = [send(wp.at[0], wp.at[4 - k], y_peer[k]) for k in (1, 2, 3)]

    def raw(b, r):
        return dot(pv[b], qv[r], NT)

    def finish_logits(b, r, value):
        value = value * (scale * LOG2E) + jnp.concatenate([count[b]] * (block // lanes), axis=1)
        top = jnp.max(value, axis=0, keepdims=True)
        expo = jnp.exp2(value - top)
        place = pl.ds(pl.multiple_of(r * block, block), block)
        coarse = expo.astype(BF16)
        ev[b, 0, :, place] = coarse
        ev[b, 1, :, place] = (expo - coarse.astype(F32)).astype(BF16)
        m_b[b, :, place] = top
        s_b[b, :, place] = jnp.sum(expo, axis=0, keepdims=True)

    def logits(b, r):
        finish_logits(b, r, raw(b, r))

    own_p.wait()
    own_q.wait()
    logits(0, 0)

    from_z, from_core = {}, {}

    def pass_on(r, sub):
        view = qv.at[r, rows(zp, core, sub)]
        from_z[r, sub] = send(view, view, z_up if sub == 0 else z_down)
        from_core[r, 0, sub] = send(view, view, other)

    def pass_over(r, sub):
        from_z[r, sub].wait_recv()
        view = qv.at[r, rows(1 - zp, core, sub)]
        from_core[r, 1, sub] = send(view, view, other)

    def have(r):
        for key in from_core:
            if key[0] == r:
                from_core[key].wait_recv()

    def to_core(b):
        for k in range(RING):
            col = pl.ds(pl.multiple_of((((z + k) % RING) * 2 + 1 - core) * strip, strip), strip)
            crossed.append(send(pv.at[b, :, col], px.at[k, b], other))

    crossed = []
    to_core(0)
    pl.loop(1, RING)(tally)
    q_right[0].wait_recv()
    q_far0 = send(qv.at[3, rows(zp, core, 0)], qv.at[2, rows(zp, core, 0)], y_peer[1])
    pass_on(3, 0)
    q_left[0].wait_recv()
    q_far1 = send(qv.at[1, rows(zp, core, 1)], qv.at[2, rows(zp, core, 1)], y_peer[3])
    pass_on(1, 1)
    p_right[0].wait_recv()
    p_far0 = send(pv.at[3, lo], pv.at[2, lo], x_peer[1])
    p_left[0].wait_recv()
    p_far1 = send(pv.at[1, hi], pv.at[2, hi], x_peer[3])
    q_right[1].wait_recv()
    pass_on(3, 1)
    q_left[1].wait_recv()
    pass_on(1, 0)
    pass_over(3, 0)
    pass_over(1, 1)
    q_far0.wait_recv()
    pass_on(2, 0)
    q_far1.wait_recv()
    pass_on(2, 1)
    pass_over(3, 1)
    pass_over(1, 0)
    have(1)
    have(3)
    pl.loop(0, 2)(lambda j: logits(0, 1 + 2 * j))
    for copy in targets:
        copy.wait_recv()
    p_right[1].wait_recv()
    p_left[1].wait_recv()
    to_core(1)
    to_core(3)

    @pl.loop(0, 6)
    def _(i):
        j = i % 3
        logits(1 + 2 * (i // 3), j + j // 2)

    pass_over(2, 0)
    pass_over(2, 1)
    have(2)
    pl.loop(0, 3)(lambda i: logits(i + i // 2, 2))
    p_far0.wait_recv()
    p_far1.wait_recv()
    to_core(2)
    value = raw(2, 0)
    for r in range(1, RING):
        later = raw(2, r)
        finish_logits(2, r - 1, value)
        value = later
    finish_logits(2, RING - 1, value)

    top = jnp.maximum(jnp.maximum(m_b[0], m_b[1]), jnp.maximum(m_b[2], m_b[3]))
    st_own[0:1, :] = top
    st_own[1:2, :] = sum(s_b[b] * jnp.exp2(m_b[b] - top) for b in range(RING))
    copies = [send(st_own, st_in.at[k], n_peer[k]) for k in range(1, N_NEG)]
    for copy in copies:
        copy.wait_recv()
    for k in range(1, N_NEG):
        top = jnp.maximum(top, st_in[k, 0:1, :])
    mass = st_own[1:2, :] * jnp.exp2(st_own[0:1, :] - top)
    for k in range(1, N_NEG):
        mass = mass + st_in[k, 1:2, :] * jnp.exp2(st_in[k, 0:1, :] - top)
    st_mid[0:1, :] = top
    st_mid[1:2, :] = mass
    copies = [send(st_mid, st_y.at[k], y_peer[k]) for k in (1, 2, 3)]
    for copy in copies:
        copy.wait_recv()
    for r in range(RING):
        mine = pl.ds(r * block, block)
        theirs = [(k, pl.ds(((r + k) % RING) * block, block)) for k in (1, 2, 3)]
        top = st_mid[0:1, mine]
        for k, place in theirs:
            top = jnp.maximum(top, st_y[k, 0:1, place])
        mass = st_mid[1:2, mine] * jnp.exp2(st_mid[0:1, mine] - top)
        for k, place in theirs:
            mass = mass + st_y[k, 1:2, place] * jnp.exp2(st_y[k, 0:1, place] - top)
        weight = wp[r, 0:1, :] / mass
        for b in range(RING):
            factor[b, :, mine] = jnp.exp2(m_b[b, :, mine] - top) * weight

    def gradient(b):
        label = (lax.broadcasted_iota(jnp.int32, (owned, block), 0) + first_id(b)).astype(F32)
        for r in range(RING):
            place = pl.ds(r * block, block)
            hit = jnp.where(label == wp[r, 1:2, :], wp[r, 0:1, :], 0.0)
            expo = ev[b, 0, :, place].astype(F32) + ev[b, 1, :, place].astype(F32)
            gv[b, :, place] = (expo * factor[b, :, place] - hit).astype(BF16)

    wide = width // 4

    def passage_part(b, n):
        col = pl.ds(pl.multiple_of(n * wide, wide), wide)
        return dot(gv[b], qv[:, :, col].reshape(RING * block, wide), NN)

    far = {}
    gradient(2)
    for n in (0, 2, 1, 3):
        col = pl.ds(n * wide, wide)
        pg[1, :, col] = passage_part(2, n).astype(BF16)
        far[n] = send(pg.at[1, :, col], pg_first.at[n], x_peer[1] if n < 2 else x_peer[3])
    grads = [send(gv.at[2], gx.at[2], other)]
    for b in (1, 3, 0):
        gradient(b)
        grads.append(send(gv.at[b], gx.at[b], other))
    for copy in grads + crossed:
        copy.wait_recv()
    for copy in crossed + [p_far0, p_far1]:
        copy.wait_send()

    def query_part(r):
        @pl.loop(0, 2 * RING)
        def _(i):
            k, level = i // 2, i % 2
            place = pl.ds(pl.multiple_of(r * block + level * mid, mid), mid)
            col = pl.ds(pl.multiple_of((((z + k) % RING) * 2 + core) * strip, strip), strip)
            mine = dot(
                gv[:, :, place].reshape(RING * owned, mid),
                pv[:, :, col].reshape(RING * owned, strip),
                TN,
            )
            theirs = dot(
                gx[:, :, place].reshape(RING * owned, mid),
                px[k].reshape(RING * owned, strip),
                TN,
            )
            out = pl.ds(pl.multiple_of(k * strip, strip), strip)
            ev[r, level, :, out] = (mine + theirs).astype(BF16)

    mid = block // 2
    quarter = mid // 2

    def span(part):
        return pl.ds(0, mid) if part is None else pl.ds(part * quarter, quarter)

    def along_y(level, k):
        return lambda rel, part: ev.at[rel, level, span(part), pl.ds(k * strip, strip)]

    def along_z(r, level):
        return lambda rel, part: ev.at[r, level, span(part), pl.ds(rel * strip, strip)]

    def spare(first, k):
        col = pl.ds(pl.multiple_of((2 * k + 1 - core) * strip, strip), strip)
        return lambda way: pv.at[first + way, :, col]

    def landing(level):
        return lambda way: q_land.at[way, pl.ds(level * mid, mid)]

    a_y = [
        RingScatter(send, y_peer[1], y_peer[3], along_y(0, k), ay1.at[k], spare(0, k)) for k in range(RING)
    ]
    b_z = [RingScatter(send, z_up, z_down, along_z(r, 1), bz1.at[r], spare(2, r)) for r in range(RING)]
    a_z = RingScatter(send, z_up, z_down, along_z(0, 0), az1, landing(0))
    b_y = RingScatter(send, y_peer[1], y_peer[3], along_y(1, 0), by1, landing(1))
    order = (2, 1, 3, 0)

    def near_part(b, n):
        col = pl.ds(n * wide, wide)
        value = passage_part(b, n)
        if (b == 1) == (n < 2):
            far[n].wait_recv()
            value = value + pg_first[n].astype(F32)
        pg[b - 1, :, col] = value.astype(BF16)
        send(pg.at[b - 1, :, col], p_land.at[0 if b == 1 else 1, :, col], x_peer[b])

    query_part(2)
    for k in order:
        a_y[k].start()
    b_z[2].start()
    for b, n in ((1, 2), (3, 0), (1, 3), (3, 1)):
        near_part(b, n)
    query_part(1)
    b_z[1].start()
    query_part(3)
    b_z[3].start()
    for k in order:
        a_y[k].middle()
    b_z[2].middle()
    query_part(0)
    b_z[0].start()
    for b, n in ((1, 0), (3, 2), (1, 1), (3, 3)):
        near_part(b, n)
    b_z[1].middle()
    b_z[3].middle()
    b_z[2].finish()
    b_y.start()
    b_z[0].middle()
    for n in range(4):
        far[n].wait_send()
        col = pl.ds(n * wide, wide)
        pg[1, :, col] = passage_part(0, n).astype(BF16)
    p_copy = pltpu.make_async_copy(pg.at[1], p_own, sems.new())
    p_copy.start()
    b_z[1].finish()
    b_z[3].finish()
    a_y[2].finish()
    a_z.start()
    a_y[1].finish()
    a_y[3].finish()
    a_z.middle()
    b_y.middle()
    a_y[0].finish()
    b_z[0].finish()
    upper = pltpu.make_async_copy(along_y(0, 0)(0, None), q_own.at[pl.ds(0, mid)], sems.new())
    lower = pltpu.make_async_copy(along_y(1, 0)(0, None), q_own.at[pl.ds(mid, mid)], sems.new())
    upper.start()
    lower.start()
    for copy in sent:
        copy.wait()
    p_copy.wait()
    upper.wait()
    lower.wait()


def add_up(q_own, q_land, p_own, p_land, q_out, p_out):
    q_out[...] = (q_own[...].astype(F32) + q_land[0].astype(F32) + q_land[1].astype(F32)).astype(BF16)
    p_out[...] = p_own[...].astype(F32) + p_land[0].astype(F32) + p_land[1].astype(F32)


def body(queries, passages, list_owner, list_row, positive, row_weight):
    block, width = queries.shape
    owned = passages.shape[0]
    lanes = list_row.shape[1]
    strip = width // N_NEG
    mid = block // 2
    any_space = pl.BlockSpec(memory_space=pl.ANY)
    vmem = pl.BlockSpec(memory_space=pltpu.VMEM)
    wide = width // 4
    scratch = [
        pltpu.VMEM((RING, block, width), BF16),
        pltpu.VMEM((RING, owned, width), BF16),
        pltpu.VMEM((RING, RING, owned, strip), BF16),
        pltpu.VMEM((RING, 2, owned, RING * block), BF16),
        pltpu.VMEM((RING, owned, RING * block), BF16),
        pltpu.VMEM((RING, owned, RING * block), BF16),
        pltpu.VMEM((3, owned, width), BF16),
        pltpu.VMEM((4, owned, wide), BF16),
        pltpu.VMEM((RING, 2, mid // 2, strip), BF16),
        pltpu.VMEM((2, mid // 2, strip), BF16),
        pltpu.VMEM((RING, 2, mid // 2, strip), BF16),
        pltpu.VMEM((2, mid // 2, strip), BF16),
        pltpu.VMEM((N_NEG, RING, RING, 1, lanes), jnp.int32),
        pltpu.VMEM((lanes, lanes), jnp.int32),
        pltpu.VMEM((RING, owned, lanes), F32),
        pltpu.VMEM((RING, 2, block), F32),
        pltpu.VMEM((RING, 1, RING * block), F32),
        pltpu.VMEM((RING, 1, RING * block), F32),
        pltpu.VMEM((2, RING * block), F32),
        pltpu.VMEM((N_NEG, 2, RING * block), F32),
        pltpu.VMEM((2, RING * block), F32),
        pltpu.VMEM((RING, 2, RING * block), F32),
        pltpu.VMEM((RING, 1, RING * block), F32),
        pltpu.SemaphoreType.DMA((SEMS,)),
    ]
    flops = 6 * RING * block * RING * owned * width
    q_own, q_land, p_own, p_land = pl.pallas_call(
        kernel,
        out_shape=(
            jax.ShapeDtypeStruct((block, strip), BF16),
            jax.ShapeDtypeStruct((2, block, strip), BF16),
            jax.ShapeDtypeStruct((owned, width), BF16),
            jax.ShapeDtypeStruct((2, owned, width), BF16),
        ),
        in_specs=[any_space, any_space, vmem, vmem, vmem, vmem],
        out_specs=(any_space,) * 4,
        scratch_shapes=scratch,
        compiler_params=pltpu.CompilerParams(
            collective_id=0, has_side_effects=True, vmem_limit_bytes=62 * 2**20
        ),
        cost_estimate=pl.CostEstimate(flops=flops, bytes_accessed=40 * 2**20, transcendentals=0),
        name="contrastive",
    )(
        queries,
        passages,
        list_owner.reshape(1, lanes),
        list_row,
        positive.reshape(1, block),
        row_weight.reshape(1, block),
    )
    steps = 4
    q_rows, p_rows = block // steps, owned // steps
    return pl.pallas_call(
        add_up,
        grid=(steps,),
        out_shape=(
            jax.ShapeDtypeStruct((block, strip), BF16),
            jax.ShapeDtypeStruct((owned, width), F32),
        ),
        in_specs=[
            pl.BlockSpec((q_rows, strip), lambda i: (i, 0)),
            pl.BlockSpec((2, q_rows, strip), lambda i: (0, i, 0)),
            pl.BlockSpec((p_rows, width), lambda i: (i, 0)),
            pl.BlockSpec((2, p_rows, width), lambda i: (0, i, 0)),
        ],
        out_specs=(
            pl.BlockSpec((q_rows, strip), lambda i: (i, 0)),
            pl.BlockSpec((p_rows, width), lambda i: (i, 0)),
        ),
        compiler_params=pltpu.CompilerParams(vmem_limit_bytes=32 * 2**20),
        name="add_up",
    )(q_own, q_land, p_own, p_land)


def solution(mesh):
    in_specs = (
        P("dp", None),
        P(("dp", "neg"), None),
        P("neg", "dp", None),
        P("neg", "dp"),
        P("dp"),
        P("dp"),
    )
    out_specs = (P("dp", "neg"), P(("dp", "neg"), None))
    return jax.shard_map(body, mesh=mesh, in_specs=in_specs, out_specs=out_specs, check_vma=False)
```

```python
import math

import jax
import jax.numpy as jnp
from jax import lax
from jax.experimental import pallas as pl
from jax.experimental.pallas import tpu as pltpu
from jax.sharding import PartitionSpec as P

MESH = pl.DeviceIdType.MESH
BF16 = jnp.bfloat16
F32 = jnp.float32
RING = 4
N_NEG = 8
SEMS = 400
LOW = -3.0e38
LOG2E = 1.0 / math.log(2.0)

NN = (((1,), (0,)), ((), ()))
NT = (((1,), (1,)), ((), ()))
TN = (((0,), (0,)), ((), ()))


def dot(a, b, dims):
    return lax.dot_general(a, b, dims, preferred_element_type=F32)


class Sems:
    def __init__(self, ref):
        self.ref = ref
        self.used = 0

    def new(self):
        self.used += 1
        assert self.used <= SEMS
        return self.ref.at[self.used - 1]


class Copy:
    def __init__(self, copy):
        self.copy, self.landed, self.left = copy, False, False
        copy.start()

    def wait_recv(self):
        if not self.landed:
            self.copy.wait_recv()
        self.landed = True

    def wait_send(self):
        if not self.left:
            self.copy.wait_send()
        self.left = True

    def wait(self):
        self.wait_recv()
        self.wait_send()


class RingScatter:
    def __init__(self, send, right, left, view, first, second):
        self.view, self.first, self.second = view, first, second
        self.up, self.down, self.send = right, left, send

    def start(self):
        self.a = self.send(self.view(2, 0), self.first.at[0], self.up)
        self.b = self.send(self.view(2, 1), self.first.at[1], self.down)

    def middle(self):
        self.a.wait_recv()
        self.b.wait_recv()
        part = self.view(1, 0)
        part[...] = (part[...].astype(F32) + self.first[0].astype(F32)).astype(BF16)
        self.c = self.send(self.view(1, None), self.second(0), self.up)
        part = self.view(3, 1)
        part[...] = (part[...].astype(F32) + self.first[1].astype(F32)).astype(BF16)
        self.d = self.send(self.view(3, None), self.second(1), self.down)

    def arrive(self):
        self.c.wait_recv()
        self.d.wait_recv()

    def finish(self):
        self.arrive()
        own = self.view(0, None)
        total = own[...].astype(F32) + self.second(0)[...].astype(F32) + self.second(1)[...].astype(F32)
        own[...] = total.astype(BF16)

    def drain(self):
        for copy in self.copies:
            copy.wait_send()


def kernel(
    q_in, p_in, owner_in, row_in, pos_in, w_in,
    q_own, q_land, p_own, p_land,
    qv, pv, px, ev, gv, gx, pg, pg_first, ay1, az1, bz1, by1,
    ids, table, count, wp, m_b, s_b, st_own, st_in, st_mid, st_y, factor,
    sem_ref,
):
    dp, neg = lax.axis_index("dp"), lax.axis_index("neg")
    x, y = dp // RING, dp % RING
    z, core = neg // 2, neg % 2
    block, width = q_in.shape
    owned = p_in.shape[0]
    strip = width // N_NEG
    scale = 3.0 / math.sqrt(width)
    sems = Sems(sem_ref)

    def device(xx, yy, zz, cc):
        return ((xx % RING) * RING + yy % RING, (zz % RING) * 2 + cc)

    x_peer = [None] + [device(x + k, y, z, core) for k in (1, 2, 3)]
    y_peer = [None] + [device(x, y + k, z, core) for k in (1, 2, 3)]
    z_up, z_down = device(x, y, z + 1, core), device(x, y, z + 3, core)
    other = device(x, y, z, 1 - core)
    n_peer = [None] + [(dp, (neg + k) % N_NEG) for k in range(1, N_NEG)]

    barrier = pltpu.get_barrier_semaphore()
    greeted = x_peer[1:] + y_peer[1:] + n_peer[1:]
    for peer in greeted:
        pl.semaphore_signal(barrier, inc=1, device_id=peer, device_id_type=MESH)
    pl.semaphore_wait(barrier, len(greeted))

    sent = []

    def send(src, dst, to):
        copy = pltpu.make_async_remote_copy(
            src, dst, sems.new(), sems.new(), device_id=to, device_id_type=MESH
        )
        sent.append(Copy(copy))
        return sent[-1]

    half = owned // 2
    lo, hi = pl.ds(0, half), pl.ds(half, half)
    piece = block // 8
    zp = z % 2

    def rows(zz, cc, sub):
        return pl.ds(pl.multiple_of(zz * (4 * piece) + cc * (2 * piece) + sub * piece, piece), piece)

    ids[neg, y, x] = owner_in[...] * owned + row_in[...]
    copies = [send(ids.at[neg, y, x], ids.at[neg, y, x], x_peer[k]) for k in (1, 2, 3)]
    p_right = [send(p_in.at[lo], pv.at[3, lo], x_peer[1])]
    p_left = [send(p_in.at[hi], pv.at[1, hi], x_peer[3])]
    own_q = pltpu.make_async_copy(q_in, qv.at[0], sems.new())
    own_p = pltpu.make_async_copy(p_in, pv.at[0], sems.new())
    own_p.start()
    own_q.start()
    for copy in copies:
        copy.wait_recv()
    copies = [send(ids.at[neg, y], ids.at[neg, y], y_peer[k]) for k in (1, 2, 3)]
    q_right = [send(q_in.at[rows(zp, core, 0)], qv.at[3, rows(zp, core, 0)], y_peer[1])]
    q_left = [send(q_in.at[rows(zp, core, 1)], qv.at[1, rows(zp, core, 1)], y_peer[3])]
    for copy in copies:
        copy.wait_recv()
    copies = [send(ids.at[neg], ids.at[neg], n_peer[k]) for k in range(1, N_NEG)]
    p_right.append(send(p_in.at[hi], pv.at[3, hi], x_peer[1]))
    p_left.append(send(p_in.at[lo], pv.at[1, lo], x_peer[3]))
    q_right.append(send(q_in.at[rows(zp, core, 1)], qv.at[3, rows(zp, core, 1)], y_peer[1]))
    q_left.append(send(q_in.at[rows(zp, core, 0)], qv.at[1, rows(zp, core, 0)], y_peer[3]))
    for copy in copies:
        copy.wait_recv()

    lanes = ids.shape[-1]

    def first_id(b):
        return ((((x + b) % RING) * RING + y) * N_NEG + neg) * owned

    def tally(b):
        name = lax.broadcasted_iota(jnp.int32, (owned, lanes), 0) + first_id(b)

        def more(i, total):
            for j in range(RING * RING):
                total = total + jnp.where(name == ids[i, j // RING, j % RING], 1.0, 0.0)
            return total

        total = lax.fori_loop(0, N_NEG, more, jnp.zeros((owned, lanes), F32))
        listed = dot(total.astype(BF16), jnp.ones((lanes, lanes), BF16), NN)
        count[b] = jnp.where(listed > 0.0, jnp.log(jnp.maximum(listed, 1.0)) * LOG2E, LOW)

    tally(0)

    for i in range(N_NEG):
        for j in range(RING * RING):
            table[pl.ds(i * RING * RING + j, 1), :] = ids[i, j // RING, j % RING]
    pos = pos_in[...]
    entry = jnp.bitwise_and(pos, lanes - 1)
    lister = pos // lanes
    listing = (
        (lister // (RING * RING)) * (RING * RING)
        + jnp.bitwise_and(lister, RING - 1) * RING
        + jnp.bitwise_and(lister // RING, RING - 1)
    )
    side = lax.broadcasted_iota(jnp.int32, (lanes, block), 0)
    chosen = jnp.where(side == listing, 1.0, 0.0).astype(BF16)
    high = (table[...] // 256).astype(F32).astype(BF16)
    low = jnp.bitwise_and(table[...], 255).astype(F32).astype(BF16)
    found = dot(high, chosen, TN) * 256.0 + dot(low, chosen, TN)
    wp[0, 0:1, :] = w_in[...] * scale
    wp[0, 1:2, :] = jnp.sum(jnp.where(side == entry, found, 0.0), axis=0, keepdims=True)
    targets = [send(wp.at[0], wp.at[4 - k], y_peer[k]) for k in (1, 2, 3)]

    def raw(b, r):
        return dot(pv[b], qv[r], NT)

    def finish_logits(b, r, value):
        value = value * (scale * LOG2E) + jnp.concatenate([count[b]] * (block // lanes), axis=1)
        top = jnp.max(value, axis=0, keepdims=True)
        expo = jnp.exp2(value - top)
        place = pl.ds(pl.multiple_of(r * block, block), block)
        coarse = expo.astype(BF16)
        ev[b, 0, :, place] = coarse
        ev[b, 1, :, place] = (expo - coarse.astype(F32)).astype(BF16)
        m_b[b, :, place] = top
        s_b[b, :, place] = jnp.sum(expo, axis=0, keepdims=True)

    def logits(b, r):
        finish_logits(b, r, raw(b, r))

    own_p.wait()
    own_q.wait()
    logits(0, 0)

    from_z, from_core = {}, {}

    def pass_on(r, sub):
        view = qv.at[r, rows(zp, core, sub)]
        from_z[r, sub] = send(view, view, z_up if sub == 0 else z_down)
        from_core[r, 0, sub] = send(view, view, other)

    def pass_over(r, sub):
        from_z[r, sub].wait_recv()
        view = qv.at[r, rows(1 - zp, core, sub)]
        from_core[r, 1, sub] = send(view, view, other)

    def have(r):
        for key in from_core:
            if key[0] == r:
                from_core[key].wait_recv()

    def to_core(b):
        for k in range(RING):
            col = pl.ds(pl.multiple_of((((z + k) % RING) * 2 + 1 - core) * strip, strip), strip)
            crossed.append(send(pv.at[b, :, col], px.at[k, b], other))

    crossed = []
    to_core(0)
    pl.loop(1, RING)(tally)
    q_right[0].wait_recv()
    q_far0 = send(qv.at[3, rows(zp, core, 0)], qv.at[2, rows(zp, core, 0)], y_peer[1])
    pass_on(3, 0)
    q_left[0].wait_recv()
    q_far1 = send(qv.at[1, rows(zp, core, 1)], qv.at[2, rows(zp, core, 1)], y_peer[3])
    pass_on(1, 1)
    p_right[0].wait_recv()
    p_far0 = send(pv.at[3, lo], pv.at[2, lo], x_peer[1])
    p_left[0].wait_recv()
    p_far1 = send(pv.at[1, hi], pv.at[2, hi], x_peer[3])
    q_right[1].wait_recv()
    pass_on(3, 1)
    q_left[1].wait_recv()
    pass_on(1, 0)
    pass_over(3, 0)
    pass_over(1, 1)
    q_far0.wait_recv()
    pass_on(2, 0)
    q_far1.wait_recv()
    pass_on(2, 1)
    pass_over(3, 1)
    pass_over(1, 0)
    have(1)
    have(3)
    pl.loop(0, 2)(lambda j: logits(0, 1 + 2 * j))
    for copy in targets:
        copy.wait_recv()
    p_right[1].wait_recv()
    p_left[1].wait_recv()
    to_core(1)
    to_core(3)

    @pl.loop(0, 6)
    def _(i):
        j = i % 3
        logits(1 + 2 * (i // 3), j + j // 2)

    pass_over(2, 0)
    pass_over(2, 1)
    have(2)
    pl.loop(0, 3)(lambda i: logits(i + i // 2, 2))
    p_far0.wait_recv()
    p_far1.wait_recv()
    to_core(2)

    def merge(pairs):
        top = pairs[0][0]
        for m, _ in pairs[1:]:
            top = jnp.maximum(top, m)
        return top, sum(mass * jnp.exp2(m - top) for m, mass in pairs)

    def within(r):
        return pl.ds(r * block, block)

    def share(r):
        top, mass = merge([(m_b[b, :, within(r)], s_b[b, :, within(r)]) for b in range(RING)])
        st_own[r, 0:1, :] = top
        st_own[r, 1:2, :] = mass
        return [send(st_own.at[r], st_in.at[k, r], n_peer[k]) for k in range(1, N_NEG)]

    def share_on(r):
        for copy in first_round[r]:
            copy.wait_recv()
        refs = [st_own.at[r]] + [st_in.at[k, r] for k in range(1, N_NEG)]
        top, mass = merge([(ref[0:1, :], ref[1:2, :]) for ref in refs])
        st_mid[r, 0:1, :] = top
        st_mid[r, 1:2, :] = mass
        return [send(st_mid.at[r], st_y.at[k, r], y_peer[k]) for k in (1, 2, 3)]

    first_round, second_round = [], []
    value = raw(2, 0)
    for r in range(1, RING):
        later = raw(2, r)
        finish_logits(2, r - 1, value)
        first_round.append(share(r - 1))
        value = later
    finish_logits(2, RING - 1, value)
    first_round.append(share(RING - 1))
    for r in range(RING):
        second_round.append(share_on(r))
    for copies in second_round:
        for copy in copies:
            copy.wait_recv()
    for r in range(RING):
        refs = [st_mid.at[r]] + [st_y.at[k, (r + k) % RING] for k in (1, 2, 3)]
        top, mass = merge([(ref[0:1, :], ref[1:2, :]) for ref in refs])
        weight = wp[r, 0:1, :] / mass
        for b in range(RING):
            factor[b, :, within(r)] = jnp.exp2(m_b[b, :, within(r)] - top) * weight

    def gradient(b):
        label = (lax.broadcasted_iota(jnp.int32, (owned, block), 0) + first_id(b)).astype(F32)
        for r in range(RING):
            place = pl.ds(r * block, block)
            hit = jnp.where(label == wp[r, 1:2, :], wp[r, 0:1, :], 0.0)
            expo = ev[b, 0, :, place].astype(F32) + ev[b, 1, :, place].astype(F32)
            gv[b, :, place] = (expo * factor[b, :, place] - hit).astype(BF16)

    wide = width // 4

    def passage_part(b, col):
        return dot(gv[b], qv[:, :, col].reshape(RING * block, col.size), NN)

    far = {}
    gradient(2)
    for start, size in ((0, 1), (4, 1), (1, 1), (5, 1), (2, 2), (6, 2)):
        col = pl.ds(start * strip, size * strip)
        pg[1, :, col] = passage_part(2, col).astype(BF16)
        to = x_peer[1] if start < 4 else x_peer[3]
        far[start] = send(pg.at[1, :, col], pg_first.at[:, col], to)
    grads = [send(gv.at[2], gx.at[2], other)]
    for b in (1, 3, 0):
        gradient(b)
        grads.append(send(gv.at[b], gx.at[b], other))
    for copy in grads + crossed:
        copy.wait_recv()
    for copy in crossed + [p_far0, p_far1]:
        copy.wait_send()

    def query_part(r):
        @pl.loop(0, 2 * RING)
        def _(i):
            k, level = i // 2, i % 2
            place = pl.ds(pl.multiple_of(r * block + level * mid, mid), mid)
            col = pl.ds(pl.multiple_of((((z + k) % RING) * 2 + core) * strip, strip), strip)
            mine = dot(
                gv[:, :, place].reshape(RING * owned, mid),
                pv[:, :, col].reshape(RING * owned, strip),
                TN,
            )
            theirs = dot(
                gx[:, :, place].reshape(RING * owned, mid),
                px[k].reshape(RING * owned, strip),
                TN,
            )
            out = pl.ds(pl.multiple_of(k * strip, strip), strip)
            ev[r, level, :, out] = (mine + theirs).astype(BF16)

    mid = block // 2
    quarter = mid // 2

    def span(part):
        return pl.ds(0, mid) if part is None else pl.ds(part * quarter, quarter)

    def along_y(level, k):
        return lambda rel, part: ev.at[rel, level, span(part), pl.ds(k * strip, strip)]

    def along_z(r, level):
        return lambda rel, part: ev.at[r, level, span(part), pl.ds(rel * strip, strip)]

    def spare(first, k):
        col = pl.ds(pl.multiple_of((2 * k + 1 - core) * strip, strip), strip)
        return lambda way: pv.at[first + way, :, col]

    def landing(level):
        return lambda way: q_land.at[way, pl.ds(level * mid, mid)]

    a_y = [
        RingScatter(send, y_peer[1], y_peer[3], along_y(0, k), ay1.at[k], spare(0, k)) for k in range(RING)
    ]
    b_z = [RingScatter(send, z_up, z_down, along_z(r, 1), bz1.at[r], spare(2, r)) for r in range(RING)]
    a_z = RingScatter(send, z_up, z_down, along_z(0, 0), az1, landing(0))
    b_y = RingScatter(send, y_peer[1], y_peer[3], along_y(1, 0), by1, landing(1))
    order = (2, 1, 3, 0)

    def near_part(b, n):
        col = pl.ds(n * wide, wide)
        value = passage_part(b, col)
        if (b == 1) == (n < 2):
            for start in (2 * n, 2 * n + 1):
                if start in far:
                    far[start].wait_recv()
            value = value + pg_first[:, col].astype(F32)
        pg[b - 1, :, col] = value.astype(BF16)
        send(pg.at[b - 1, :, col], p_land.at[0 if b == 1 else 1, :, col], x_peer[b])

    query_part(2)
    for k in order:
        a_y[k].start()
    b_z[2].start()
    for b, n in ((1, 2), (3, 0), (1, 3), (3, 1)):
        near_part(b, n)
    b_z[2].middle()
    query_part(1)
    b_z[1].start()
    query_part(3)
    b_z[3].start()
    b_z[2].finish()
    b_y.start()
    for k in order:
        a_y[k].middle()
    b_z[1].middle()
    query_part(0)
    b_z[0].start()
    b_z[3].middle()
    for b, n in ((1, 0), (3, 2), (1, 1), (3, 3)):
        near_part(b, n)
    b_z[1].finish()
    b_z[0].middle()
    b_z[3].finish()
    b_y.middle()
    for copy in far.values():
        copy.wait_send()
    for n in range(4):
        col = pl.ds(n * wide, wide)
        pg[1, :, col] = passage_part(0, col).astype(BF16)
    p_copy = pltpu.make_async_copy(pg.at[1], p_own, sems.new())
    p_copy.start()
    b_z[0].finish()
    a_y[2].finish()
    a_z.start()
    a_y[1].finish()
    a_y[3].finish()
    a_z.middle()
    a_y[0].finish()
    upper = pltpu.make_async_copy(along_y(0, 0)(0, None), q_own.at[pl.ds(0, mid)], sems.new())
    lower = pltpu.make_async_copy(along_y(1, 0)(0, None), q_own.at[pl.ds(mid, mid)], sems.new())
    upper.start()
    lower.start()
    for copy in sent:
        copy.wait()
    p_copy.wait()
    upper.wait()
    lower.wait()


def add_up(q_own, q_land, p_own, p_land, q_out, p_out):
    q_out[...] = (q_own[...].astype(F32) + q_land[0].astype(F32) + q_land[1].astype(F32)).astype(BF16)
    p_out[...] = p_own[...].astype(F32) + p_land[0].astype(F32) + p_land[1].astype(F32)


def body(queries, passages, list_owner, list_row, positive, row_weight):
    block, width = queries.shape
    owned = passages.shape[0]
    lanes = list_row.shape[1]
    strip = width // N_NEG
    mid = block // 2
    any_space = pl.BlockSpec(memory_space=pl.ANY)
    vmem = pl.BlockSpec(memory_space=pltpu.VMEM)
    wide = width // 4
    scratch = [
        pltpu.VMEM((RING, block, width), BF16),
        pltpu.VMEM((RING, owned, width), BF16),
        pltpu.VMEM((RING, RING, owned, strip), BF16),
        pltpu.VMEM((RING, 2, owned, RING * block), BF16),
        pltpu.VMEM((RING, owned, RING * block), BF16),
        pltpu.VMEM((RING, owned, RING * block), BF16),
        pltpu.VMEM((3, owned, width), BF16),
        pltpu.VMEM((owned, width), BF16),
        pltpu.VMEM((RING, 2, mid // 2, strip), BF16),
        pltpu.VMEM((2, mid // 2, strip), BF16),
        pltpu.VMEM((RING, 2, mid // 2, strip), BF16),
        pltpu.VMEM((2, mid // 2, strip), BF16),
        pltpu.VMEM((N_NEG, RING, RING, 1, lanes), jnp.int32),
        pltpu.VMEM((lanes, lanes), jnp.int32),
        pltpu.VMEM((RING, owned, lanes), F32),
        pltpu.VMEM((RING, 2, block), F32),
        pltpu.VMEM((RING, 1, RING * block), F32),
        pltpu.VMEM((RING, 1, RING * block), F32),
        pltpu.VMEM((RING, 2, block), F32),
        pltpu.VMEM((N_NEG, RING, 2, block), F32),
        pltpu.VMEM((RING, 2, block), F32),
        pltpu.VMEM((RING, RING, 2, block), F32),
        pltpu.VMEM((RING, 1, RING * block), F32),
        pltpu.SemaphoreType.DMA((SEMS,)),
    ]
    flops = 6 * RING * block * RING * owned * width
    q_own, q_land, p_own, p_land = pl.pallas_call(
        kernel,
        out_shape=(
            jax.ShapeDtypeStruct((block, strip), BF16),
            jax.ShapeDtypeStruct((2, block, strip), BF16),
            jax.ShapeDtypeStruct((owned, width), BF16),
            jax.ShapeDtypeStruct((2, owned, width), BF16),
        ),
        in_specs=[any_space, any_space, vmem, vmem, vmem, vmem],
        out_specs=(any_space,) * 4,
        scratch_shapes=scratch,
        compiler_params=pltpu.CompilerParams(
            collective_id=0, has_side_effects=True, vmem_limit_bytes=62 * 2**20
        ),
        cost_estimate=pl.CostEstimate(flops=flops, bytes_accessed=40 * 2**20, transcendentals=0),
        name="contrastive",
    )(
        queries,
        passages,
        list_owner.reshape(1, lanes),
        list_row,
        positive.reshape(1, block),
        row_weight.reshape(1, block),
    )
    steps = 2
    q_rows, p_rows = block // steps, owned // steps
    return pl.pallas_call(
        add_up,
        grid=(steps,),
        out_shape=(
            jax.ShapeDtypeStruct((block, strip), BF16),
            jax.ShapeDtypeStruct((owned, width), F32),
        ),
        in_specs=[
            pl.BlockSpec((q_rows, strip), lambda i: (i, 0)),
            pl.BlockSpec((2, q_rows, strip), lambda i: (0, i, 0)),
            pl.BlockSpec((p_rows, width), lambda i: (i, 0)),
            pl.BlockSpec((2, p_rows, width), lambda i: (0, i, 0)),
        ],
        out_specs=(
            pl.BlockSpec((q_rows, strip), lambda i: (i, 0)),
            pl.BlockSpec((p_rows, width), lambda i: (i, 0)),
        ),
        compiler_params=pltpu.CompilerParams(vmem_limit_bytes=60 * 2**20),
        name="add_up",
    )(q_own, q_land, p_own, p_land)


def solution(mesh):
    in_specs = (
        P("dp", None),
        P(("dp", "neg"), None),
        P("neg", "dp", None),
        P("neg", "dp"),
        P("dp"),
        P("dp"),
    )
    out_specs = (P("dp", "neg"), P(("dp", "neg"), None))
    return jax.shard_map(body, mesh=mesh, in_specs=in_specs, out_specs=out_specs, check_vma=False)
```

```python
import math

import jax
import jax.numpy as jnp
from jax import lax
from jax.experimental import pallas as pl
from jax.experimental.pallas import tpu as pltpu
from jax.sharding import PartitionSpec as P

MESH = pl.DeviceIdType.MESH
BF16 = jnp.bfloat16
F32 = jnp.float32
RING = 4
N_NEG = 8
SEMS = 400
LOW = -3.0e38
LOG2E = 1.0 / math.log(2.0)

NN = (((1,), (0,)), ((), ()))
NT = (((1,), (1,)), ((), ()))
TN = (((0,), (0,)), ((), ()))


def dot(a, b, dims):
    return lax.dot_general(a, b, dims, preferred_element_type=F32)


class Sems:
    def __init__(self, ref):
        self.ref = ref
        self.used = 0

    def new(self):
        self.used += 1
        assert self.used <= SEMS
        return self.ref.at[self.used - 1]


class Copy:
    def __init__(self, copy):
        self.copy, self.landed, self.left = copy, False, False
        copy.start()

    def wait_recv(self):
        if not self.landed:
            self.copy.wait_recv()
        self.landed = True

    def wait_send(self):
        if not self.left:
            self.copy.wait_send()
        self.left = True

    def wait(self):
        self.wait_recv()
        self.wait_send()


class RingScatter:
    def __init__(self, send, right, left, view, first, second):
        self.view, self.first, self.second = view, first, second
        self.up, self.down, self.send = right, left, send

    def start(self):
        self.a = self.send(self.view(2, 0), self.first.at[0], self.up)
        self.b = self.send(self.view(2, 1), self.first.at[1], self.down)

    def middle(self):
        self.a.wait_recv()
        self.b.wait_recv()
        part = self.view(1, 0)
        part[...] = (part[...].astype(F32) + self.first[0].astype(F32)).astype(BF16)
        self.c = self.send(self.view(1, None), self.second(0), self.up)
        part = self.view(3, 1)
        part[...] = (part[...].astype(F32) + self.first[1].astype(F32)).astype(BF16)
        self.d = self.send(self.view(3, None), self.second(1), self.down)

    def arrive(self):
        self.c.wait_recv()
        self.d.wait_recv()

    def finish(self):
        self.arrive()
        own = self.view(0, None)
        total = own[...].astype(F32) + self.second(0)[...].astype(F32) + self.second(1)[...].astype(F32)
        own[...] = total.astype(BF16)

    def drain(self):
        for copy in self.copies:
            copy.wait_send()


def kernel(
    q_in, p_in, owner_in, row_in, pos_in, w_in,
    q_own, q_land, p_own, p_land,
    qv, pv, px, ev, gv, gx, pg, pg_first, ay1, az1, bz1, by1,
    ids, table, count, wp, m_b, s_b, st_own, st_in, st_mid, st_y, factor,
    sem_ref,
):
    dp, neg = lax.axis_index("dp"), lax.axis_index("neg")
    x, y = dp // RING, dp % RING
    z, core = neg // 2, neg % 2
    block, width = q_in.shape
    owned = p_in.shape[0]
    strip = width // N_NEG
    scale = 3.0 / math.sqrt(width)
    sems = Sems(sem_ref)

    def device(xx, yy, zz, cc):
        return ((xx % RING) * RING + yy % RING, (zz % RING) * 2 + cc)

    x_peer = [None] + [device(x + k, y, z, core) for k in (1, 2, 3)]
    y_peer = [None] + [device(x, y + k, z, core) for k in (1, 2, 3)]
    z_up, z_down = device(x, y, z + 1, core), device(x, y, z + 3, core)
    other = device(x, y, z, 1 - core)
    n_peer = [None] + [(dp, (neg + k) % N_NEG) for k in range(1, N_NEG)]

    barrier = pltpu.get_barrier_semaphore()
    greeted = x_peer[1:] + y_peer[1:] + n_peer[1:]
    for peer in greeted:
        pl.semaphore_signal(barrier, inc=1, device_id=peer, device_id_type=MESH)
    pl.semaphore_wait(barrier, len(greeted))

    sent = []

    def send(src, dst, to):
        copy = pltpu.make_async_remote_copy(
            src, dst, sems.new(), sems.new(), device_id=to, device_id_type=MESH
        )
        sent.append(Copy(copy))
        return sent[-1]

    half = owned // 2
    lo, hi = pl.ds(0, half), pl.ds(half, half)
    piece = block // 8
    zp = z % 2

    def rows(zz, cc, sub):
        return pl.ds(pl.multiple_of(zz * (4 * piece) + cc * (2 * piece) + sub * piece, piece), piece)

    ids[neg, y, x] = owner_in[...] * owned + row_in[...]
    copies = [send(ids.at[neg, y, x], ids.at[neg, y, x], x_peer[k]) for k in (1, 2, 3)]
    p_right = [send(p_in.at[lo], pv.at[3, lo], x_peer[1])]
    p_left = [send(p_in.at[hi], pv.at[1, hi], x_peer[3])]
    own_q = pltpu.make_async_copy(q_in, qv.at[0], sems.new())
    own_p = pltpu.make_async_copy(p_in, pv.at[0], sems.new())
    own_p.start()
    own_q.start()
    for copy in copies:
        copy.wait_recv()
    copies = [send(ids.at[neg, y], ids.at[neg, y], y_peer[k]) for k in (1, 2, 3)]
    q_right = [send(q_in.at[rows(zp, core, 0)], qv.at[3, rows(zp, core, 0)], y_peer[1])]
    q_left = [send(q_in.at[rows(zp, core, 1)], qv.at[1, rows(zp, core, 1)], y_peer[3])]
    for copy in copies:
        copy.wait_recv()
    copies = [send(ids.at[neg], ids.at[neg], n_peer[k]) for k in range(1, N_NEG)]
    p_right.append(send(p_in.at[hi], pv.at[3, hi], x_peer[1]))
    p_left.append(send(p_in.at[lo], pv.at[1, lo], x_peer[3]))
    q_right.append(send(q_in.at[rows(zp, core, 1)], qv.at[3, rows(zp, core, 1)], y_peer[1]))
    q_left.append(send(q_in.at[rows(zp, core, 0)], qv.at[1, rows(zp, core, 0)], y_peer[3]))
    for copy in copies:
        copy.wait_recv()

    lanes = ids.shape[-1]

    def first_id(b):
        return ((((x + b) % RING) * RING + y) * N_NEG + neg) * owned

    def tally(b):
        name = lax.broadcasted_iota(jnp.int32, (owned, lanes), 0) + first_id(b)

        def more(i, total):
            for j in range(RING * RING):
                total = total + jnp.where(name == ids[i, j // RING, j % RING], 1.0, 0.0)
            return total

        total = lax.fori_loop(0, N_NEG, more, jnp.zeros((owned, lanes), F32))
        listed = dot(total.astype(BF16), jnp.ones((lanes, lanes), BF16), NN)
        count[b] = jnp.where(listed > 0.0, jnp.log(jnp.maximum(listed, 1.0)) * LOG2E, LOW)

    tally(0)

    for i in range(N_NEG):
        for j in range(RING * RING):
            table[pl.ds(i * RING * RING + j, 1), :] = ids[i, j // RING, j % RING]
    pos = pos_in[...]
    entry = jnp.bitwise_and(pos, lanes - 1)
    lister = pos // lanes
    listing = (
        (lister // (RING * RING)) * (RING * RING)
        + jnp.bitwise_and(lister, RING - 1) * RING
        + jnp.bitwise_and(lister // RING, RING - 1)
    )
    side = lax.broadcasted_iota(jnp.int32, (lanes, block), 0)
    chosen = jnp.where(side == listing, 1.0, 0.0).astype(BF16)
    high = (table[...] // 256).astype(F32).astype(BF16)
    low = jnp.bitwise_and(table[...], 255).astype(F32).astype(BF16)
    found = dot(high, chosen, TN) * 256.0 + dot(low, chosen, TN)
    wp[0, 0:1, :] = w_in[...] * scale
    wp[0, 1:2, :] = jnp.sum(jnp.where(side == entry, found, 0.0), axis=0, keepdims=True)
    targets = [send(wp.at[0], wp.at[4 - k], y_peer[k]) for k in (1, 2, 3)]

    def raw(b, r):
        return dot(pv[b], qv[r], NT)

    def finish_logits(b, r, value):
        value = value * (scale * LOG2E) + jnp.concatenate([count[b]] * (block // lanes), axis=1)
        top = jnp.max(value, axis=0, keepdims=True)
        expo = jnp.exp2(value - top)
        place = pl.ds(pl.multiple_of(r * block, block), block)
        coarse = expo.astype(BF16)
        ev[b, 0, :, place] = coarse
        ev[b, 1, :, place] = (expo - coarse.astype(F32)).astype(BF16)
        m_b[b, :, place] = top
        s_b[b, :, place] = jnp.sum(expo, axis=0, keepdims=True)

    def logits(b, r):
        finish_logits(b, r, raw(b, r))

    own_p.wait()
    own_q.wait()
    logits(0, 0)

    from_z, from_core = {}, {}

    def pass_on(r, sub):
        view = qv.at[r, rows(zp, core, sub)]
        from_z[r, sub] = send(view, view, z_up if sub == 0 else z_down)
        from_core[r, 0, sub] = send(view, view, other)

    def pass_over(r, sub):
        from_z[r, sub].wait_recv()
        view = qv.at[r, rows(1 - zp, core, sub)]
        from_core[r, 1, sub] = send(view, view, other)

    def have(r):
        for key in from_core:
            if key[0] == r:
                from_core[key].wait_recv()

    def to_core(b):
        for k in range(RING):
            col = pl.ds(pl.multiple_of((((z + k) % RING) * 2 + 1 - core) * strip, strip), strip)
            crossed.append(send(pv.at[b, :, col], px.at[k, b], other))

    crossed = []
    to_core(0)
    pl.loop(1, RING)(tally)
    q_right[0].wait_recv()
    q_far0 = send(qv.at[3, rows(zp, core, 0)], qv.at[2, rows(zp, core, 0)], y_peer[1])
    pass_on(3, 0)
    q_left[0].wait_recv()
    q_far1 = send(qv.at[1, rows(zp, core, 1)], qv.at[2, rows(zp, core, 1)], y_peer[3])
    pass_on(1, 1)
    p_right[0].wait_recv()
    p_far0 = send(pv.at[3, lo], pv.at[2, lo], x_peer[1])
    p_left[0].wait_recv()
    p_far1 = send(pv.at[1, hi], pv.at[2, hi], x_peer[3])
    q_right[1].wait_recv()
    pass_on(3, 1)
    q_left[1].wait_recv()
    pass_on(1, 0)
    pass_over(3, 0)
    pass_over(1, 1)
    q_far0.wait_recv()
    pass_on(2, 0)
    q_far1.wait_recv()
    pass_on(2, 1)
    pass_over(3, 1)
    pass_over(1, 0)
    have(1)
    have(3)
    pl.loop(0, 2)(lambda j: logits(0, 1 + 2 * j))
    for copy in targets:
        copy.wait_recv()
    p_right[1].wait_recv()
    p_left[1].wait_recv()
    to_core(1)
    to_core(3)

    @pl.loop(0, 6)
    def _(i):
        j = i % 3
        logits(1 + 2 * (i // 3), j + j // 2)

    pass_over(2, 0)
    pass_over(2, 1)
    have(2)
    pl.loop(0, 3)(lambda i: logits(i + i // 2, 2))
    p_far0.wait_recv()
    p_far1.wait_recv()
    to_core(2)

    def merge(pairs):
        top = pairs[0][0]
        for m, _ in pairs[1:]:
            top = jnp.maximum(top, m)
        return top, sum(mass * jnp.exp2(m - top) for m, mass in pairs)

    def within(r):
        return pl.ds(r * block, block)

    def share(r):
        top, mass = merge([(m_b[b, :, within(r)], s_b[b, :, within(r)]) for b in range(RING)])
        st_own[r, 0:1, :] = top
        st_own[r, 1:2, :] = mass
        return [send(st_own.at[r], st_in.at[k, r], n_peer[k]) for k in range(1, N_NEG)]

    def share_on(r):
        for copy in first_round[r]:
            copy.wait_recv()
        refs = [st_own.at[r]] + [st_in.at[k, r] for k in range(1, N_NEG)]
        top, mass = merge([(ref[0:1, :], ref[1:2, :]) for ref in refs])
        st_mid[r, 0:1, :] = top
        st_mid[r, 1:2, :] = mass
        return [send(st_mid.at[r], st_y.at[k, r], y_peer[k]) for k in (1, 2, 3)]

    first_round, second_round = [], []
    value = raw(2, 0)
    for r in range(1, RING):
        later = raw(2, r)
        finish_logits(2, r - 1, value)
        first_round.append(share(r - 1))
        value = later
    finish_logits(2, RING - 1, value)
    first_round.append(share(RING - 1))
    for r in range(RING):
        second_round.append(share_on(r))
    for copies in second_round:
        for copy in copies:
            copy.wait_recv()
    for r in range(RING):
        refs = [st_mid.at[r]] + [st_y.at[k, (r + k) % RING] for k in (1, 2, 3)]
        top, mass = merge([(ref[0:1, :], ref[1:2, :]) for ref in refs])
        weight = wp[r, 0:1, :] / mass
        for b in range(RING):
            factor[b, :, within(r)] = jnp.exp2(m_b[b, :, within(r)] - top) * weight

    def gradient(b):
        label = (lax.broadcasted_iota(jnp.int32, (owned, block), 0) + first_id(b)).astype(F32)
        for r in range(RING):
            place = pl.ds(r * block, block)
            hit = jnp.where(label == wp[r, 1:2, :], wp[r, 0:1, :], 0.0)
            expo = ev[b, 0, :, place].astype(F32) + ev[b, 1, :, place].astype(F32)
            gv[b, :, place] = (expo * factor[b, :, place] - hit).astype(BF16)

    wide = width // 4

    def passage_part(b, col):
        return dot(gv[b], qv[:, :, col].reshape(RING * block, col.size), NN)

    far = {}
    gradient(2)
    for start, size in ((0, 1), (4, 1), (1, 1), (5, 1), (2, 2), (6, 2)):
        col = pl.ds(start * strip, size * strip)
        pg[1, :, col] = passage_part(2, col).astype(BF16)
        to = x_peer[1] if start < 4 else x_peer[3]
        far[start] = send(pg.at[1, :, col], pg_first.at[:, col], to)
    grads = [send(gv.at[2], gx.at[2], other)]
    for b in (1, 3, 0):
        gradient(b)
        grads.append(send(gv.at[b], gx.at[b], other))
    for copy in grads + crossed:
        copy.wait_recv()
    for copy in crossed + [p_far0, p_far1]:
        copy.wait_send()

    def query_part(r):
        @pl.loop(0, 2 * RING)
        def _(i):
            k, level = i // 2, i % 2
            place = pl.ds(pl.multiple_of(r * block + level * mid, mid), mid)
            col = pl.ds(pl.multiple_of((((z + k) % RING) * 2 + core) * strip, strip), strip)
            mine = dot(
                gv[:, :, place].reshape(RING * owned, mid),
                pv[:, :, col].reshape(RING * owned, strip),
                TN,
            )
            theirs = dot(
                gx[:, :, place].reshape(RING * owned, mid),
                px[k].reshape(RING * owned, strip),
                TN,
            )
            out = pl.ds(pl.multiple_of(k * strip, strip), strip)
            ev[r, level, :, out] = (mine + theirs).astype(BF16)

    mid = block // 2
    quarter = mid // 2

    def span(part):
        return pl.ds(0, mid) if part is None else pl.ds(part * quarter, quarter)

    def along_y(level, k):
        return lambda rel, part: ev.at[rel, level, span(part), pl.ds(k * strip, strip)]

    def along_z(r, level):
        return lambda rel, part: ev.at[r, level, span(part), pl.ds(rel * strip, strip)]

    def spare(first, k):
        col = pl.ds(pl.multiple_of((2 * k + 1 - core) * strip, strip), strip)
        return lambda way: pv.at[first + way, :, col]

    def landing(level):
        return lambda way: q_land.at[way, pl.ds(level * mid, mid)]

    a_y = [
        RingScatter(send, y_peer[1], y_peer[3], along_y(0, k), ay1.at[k], spare(0, k)) for k in range(RING)
    ]
    b_z = [RingScatter(send, z_up, z_down, along_z(r, 1), bz1.at[r], spare(2, r)) for r in range(RING)]
    a_z = RingScatter(send, z_up, z_down, along_z(0, 0), az1, landing(0))
    b_y = RingScatter(send, y_peer[1], y_peer[3], along_y(1, 0), by1, landing(1))
    order = (2, 1, 3, 0)

    def near_part(b, n):
        col = pl.ds(n * wide, wide)
        value = passage_part(b, col)
        if (b == 1) == (n < 2):
            for start in (2 * n, 2 * n + 1):
                if start in far:
                    far[start].wait_recv()
            value = value + pg_first[:, col].astype(F32)
        pg[b - 1, :, col] = value.astype(BF16)
        send(pg.at[b - 1, :, col], p_land.at[0 if b == 1 else 1, :, col], x_peer[b])

    query_part(2)
    for k in order:
        a_y[k].start()
    b_z[2].start()
    for b, n in ((1, 2), (3, 0), (1, 3), (3, 1)):
        near_part(b, n)
    b_z[2].middle()
    query_part(1)
    b_z[1].start()
    query_part(3)
    b_z[3].start()
    b_z[2].finish()
    b_y.start()
    for k in order:
        a_y[k].middle()
    b_z[1].middle()
    query_part(0)
    b_z[0].start()
    b_z[3].middle()
    for b, n in ((1, 0), (3, 2), (1, 1), (3, 3)):
        near_part(b, n)
    b_z[1].finish()
    b_z[0].middle()
    b_z[3].finish()
    b_y.middle()
    a_y[2].finish()
    a_z.start()
    for copy in far.values():
        copy.wait_send()
    for n in range(4):
        col = pl.ds(n * wide, wide)
        pg[1, :, col] = passage_part(0, col).astype(BF16)
    p_copy = pltpu.make_async_copy(pg.at[1], p_own, sems.new())
    p_copy.start()
    b_z[0].finish()
    a_y[1].finish()
    a_y[3].finish()
    a_z.middle()
    a_y[0].finish()
    upper = pltpu.make_async_copy(along_y(0, 0)(0, None), q_own.at[pl.ds(0, mid)], sems.new())
    lower = pltpu.make_async_copy(along_y(1, 0)(0, None), q_own.at[pl.ds(mid, mid)], sems.new())
    upper.start()
    lower.start()
    for copy in sent:
        copy.wait()
    p_copy.wait()
    upper.wait()
    lower.wait()


def add_up(q_own, q_land, p_own, p_land, q_out, p_out):
    q_out[...] = (q_own[...].astype(F32) + q_land[0].astype(F32) + q_land[1].astype(F32)).astype(BF16)
    p_out[...] = p_own[...].astype(F32) + p_land[0].astype(F32) + p_land[1].astype(F32)


def body(queries, passages, list_owner, list_row, positive, row_weight):
    block, width = queries.shape
    owned = passages.shape[0]
    lanes = list_row.shape[1]
    strip = width // N_NEG
    mid = block // 2
    any_space = pl.BlockSpec(memory_space=pl.ANY)
    vmem = pl.BlockSpec(memory_space=pltpu.VMEM)
    wide = width // 4
    scratch = [
        pltpu.VMEM((RING, block, width), BF16),
        pltpu.VMEM((RING, owned, width), BF16),
        pltpu.VMEM((RING, RING, owned, strip), BF16),
        pltpu.VMEM((RING, 2, owned, RING * block), BF16),
        pltpu.VMEM((RING, owned, RING * block), BF16),
        pltpu.VMEM((RING, owned, RING * block), BF16),
        pltpu.VMEM((3, owned, width), BF16),
        pltpu.VMEM((owned, width), BF16),
        pltpu.VMEM((RING, 2, mid // 2, strip), BF16),
        pltpu.VMEM((2, mid // 2, strip), BF16),
        pltpu.VMEM((RING, 2, mid // 2, strip), BF16),
        pltpu.VMEM((2, mid // 2, strip), BF16),
        pltpu.VMEM((N_NEG, RING, RING, 1, lanes), jnp.int32),
        pltpu.VMEM((lanes, lanes), jnp.int32),
        pltpu.VMEM((RING, owned, lanes), F32),
        pltpu.VMEM((RING, 2, block), F32),
        pltpu.VMEM((RING, 1, RING * block), F32),
        pltpu.VMEM((RING, 1, RING * block), F32),
        pltpu.VMEM((RING, 2, block), F32),
        pltpu.VMEM((N_NEG, RING, 2, block), F32),
        pltpu.VMEM((RING, 2, block), F32),
        pltpu.VMEM((RING, RING, 2, block), F32),
        pltpu.VMEM((RING, 1, RING * block), F32),
        pltpu.SemaphoreType.DMA((SEMS,)),
    ]
    flops = 6 * RING * block * RING * owned * width
    q_own, q_land, p_own, p_land = pl.pallas_call(
        kernel,
        out_shape=(
            jax.ShapeDtypeStruct((block, strip), BF16),
            jax.ShapeDtypeStruct((2, block, strip), BF16),
            jax.ShapeDtypeStruct((owned, width), BF16),
            jax.ShapeDtypeStruct((2, owned, width), BF16),
        ),
        in_specs=[any_space, any_space, vmem, vmem, vmem, vmem],
        out_specs=(any_space,) * 4,
        scratch_shapes=scratch,
        compiler_params=pltpu.CompilerParams(
            collective_id=0, has_side_effects=True, vmem_limit_bytes=62 * 2**20
        ),
        cost_estimate=pl.CostEstimate(flops=flops, bytes_accessed=40 * 2**20, transcendentals=0),
        name="contrastive",
    )(
        queries,
        passages,
        list_owner.reshape(1, lanes),
        list_row,
        positive.reshape(1, block),
        row_weight.reshape(1, block),
    )
    steps = 2
    q_rows, p_rows = block // steps, owned // steps
    return pl.pallas_call(
        add_up,
        grid=(steps,),
        out_shape=(
            jax.ShapeDtypeStruct((block, strip), BF16),
            jax.ShapeDtypeStruct((owned, width), F32),
        ),
        in_specs=[
            pl.BlockSpec((q_rows, strip), lambda i: (i, 0)),
            pl.BlockSpec((2, q_rows, strip), lambda i: (0, i, 0)),
            pl.BlockSpec((p_rows, width), lambda i: (i, 0)),
            pl.BlockSpec((2, p_rows, width), lambda i: (0, i, 0)),
        ],
        out_specs=(
            pl.BlockSpec((q_rows, strip), lambda i: (i, 0)),
            pl.BlockSpec((p_rows, width), lambda i: (i, 0)),
        ),
        compiler_params=pltpu.CompilerParams(vmem_limit_bytes=60 * 2**20),
        name="add_up",
    )(q_own, q_land, p_own, p_land)


def solution(mesh):
    in_specs = (
        P("dp", None),
        P(("dp", "neg"), None),
        P("neg", "dp", None),
        P("neg", "dp"),
        P("dp"),
        P("dp"),
    )
    out_specs = (P("dp", "neg"), P(("dp", "neg"), None))
    return jax.shard_map(body, mesh=mesh, in_specs=in_specs, out_specs=out_specs, check_vma=False)
```

```python
import math

import jax
import jax.numpy as jnp
from jax import lax
from jax.experimental import pallas as pl
from jax.experimental.pallas import tpu as pltpu
from jax.sharding import PartitionSpec as P

MESH = pl.DeviceIdType.MESH
BF16 = jnp.bfloat16
F32 = jnp.float32
RING = 4
N_NEG = 8
SEMS = 400
LOW = -3.0e38
LOG2E = 1.0 / math.log(2.0)

NN = (((1,), (0,)), ((), ()))
NT = (((1,), (1,)), ((), ()))
TN = (((0,), (0,)), ((), ()))


def dot(a, b, dims):
    return lax.dot_general(a, b, dims, preferred_element_type=F32)


class Sems:
    def __init__(self, ref):
        self.ref = ref
        self.used = 0

    def new(self):
        self.used += 1
        assert self.used <= SEMS
        return self.ref.at[self.used - 1]


class Copy:
    def __init__(self, copy):
        self.copy, self.landed, self.left = copy, False, False
        copy.start()

    def wait_recv(self):
        if not self.landed:
            self.copy.wait_recv()
        self.landed = True

    def wait_send(self):
        if not self.left:
            self.copy.wait_send()
        self.left = True

    def wait(self):
        self.wait_recv()
        self.wait_send()


class RingScatter:
    def __init__(self, send, right, left, view, first, second):
        self.view, self.first, self.second = view, first, second
        self.up, self.down, self.send = right, left, send

    def start(self):
        self.a = self.send(self.view(2, 0), self.first.at[0], self.up)
        self.b = self.send(self.view(2, 1), self.first.at[1], self.down)

    def middle(self):
        self.a.wait_recv()
        self.b.wait_recv()
        part = self.view(1, 0)
        part[...] = (part[...].astype(F32) + self.first[0].astype(F32)).astype(BF16)
        self.c = self.send(self.view(1, None), self.second(0), self.up)
        part = self.view(3, 1)
        part[...] = (part[...].astype(F32) + self.first[1].astype(F32)).astype(BF16)
        self.d = self.send(self.view(3, None), self.second(1), self.down)

    def arrive(self):
        self.c.wait_recv()
        self.d.wait_recv()

    def finish(self):
        self.arrive()
        own = self.view(0, None)
        total = own[...].astype(F32) + self.second(0)[...].astype(F32) + self.second(1)[...].astype(F32)
        own[...] = total.astype(BF16)

    def drain(self):
        for copy in self.copies:
            copy.wait_send()


def kernel(
    q_in, p_in, owner_in, row_in, pos_in, w_in,
    q_own, q_land, p_own, p_land,
    qv, pv, px, ev, gv, gx, pg, pg_first, ay1, az1, bz1, by1,
    ids, table, count, wp, m_b, s_b, r_b, st_own, st_in, st_mid, st_y, factor,
    sem_ref,
):
    dp, neg = lax.axis_index("dp"), lax.axis_index("neg")
    x, y = dp // RING, dp % RING
    z, core = neg // 2, neg % 2
    block, width = q_in.shape
    owned = p_in.shape[0]
    strip = width // N_NEG
    scale = 3.0 / math.sqrt(width)
    sems = Sems(sem_ref)

    def device(xx, yy, zz, cc):
        return ((xx % RING) * RING + yy % RING, (zz % RING) * 2 + cc)

    x_peer = [None] + [device(x + k, y, z, core) for k in (1, 2, 3)]
    y_peer = [None] + [device(x, y + k, z, core) for k in (1, 2, 3)]
    z_up, z_down = device(x, y, z + 1, core), device(x, y, z + 3, core)
    other = device(x, y, z, 1 - core)
    n_peer = [None] + [(dp, (neg + k) % N_NEG) for k in range(1, N_NEG)]

    barrier = pltpu.get_barrier_semaphore()
    greeted = x_peer[1:] + y_peer[1:] + n_peer[1:]
    for peer in greeted:
        pl.semaphore_signal(barrier, inc=1, device_id=peer, device_id_type=MESH)
    pl.semaphore_wait(barrier, len(greeted))

    sent = []

    def send(src, dst, to):
        copy = pltpu.make_async_remote_copy(
            src, dst, sems.new(), sems.new(), device_id=to, device_id_type=MESH
        )
        sent.append(Copy(copy))
        return sent[-1]

    half = owned // 2
    lo, hi = pl.ds(0, half), pl.ds(half, half)
    piece = block // 8
    zp = z % 2

    def rows(zz, cc, sub):
        return pl.ds(pl.multiple_of(zz * (4 * piece) + cc * (2 * piece) + sub * piece, piece), piece)

    ids[neg, y, x] = owner_in[...] * owned + row_in[...]
    copies = [send(ids.at[neg, y, x], ids.at[neg, y, x], x_peer[k]) for k in (1, 2, 3)]
    p_right = [send(p_in.at[lo], pv.at[3, lo], x_peer[1])]
    p_left = [send(p_in.at[hi], pv.at[1, hi], x_peer[3])]
    own_q = pltpu.make_async_copy(q_in, qv.at[0], sems.new())
    own_p = pltpu.make_async_copy(p_in, pv.at[0], sems.new())
    own_p.start()
    own_q.start()
    for copy in copies:
        copy.wait_recv()
    copies = [send(ids.at[neg, y], ids.at[neg, y], y_peer[k]) for k in (1, 2, 3)]
    q_right = [send(q_in.at[rows(zp, core, 0)], qv.at[3, rows(zp, core, 0)], y_peer[1])]
    q_left = [send(q_in.at[rows(zp, core, 1)], qv.at[1, rows(zp, core, 1)], y_peer[3])]
    for copy in copies:
        copy.wait_recv()
    copies = [send(ids.at[neg], ids.at[neg], n_peer[k]) for k in range(1, N_NEG)]
    p_right.append(send(p_in.at[hi], pv.at[3, hi], x_peer[1]))
    p_left.append(send(p_in.at[lo], pv.at[1, lo], x_peer[3]))
    q_right.append(send(q_in.at[rows(zp, core, 1)], qv.at[3, rows(zp, core, 1)], y_peer[1]))
    q_left.append(send(q_in.at[rows(zp, core, 0)], qv.at[1, rows(zp, core, 0)], y_peer[3]))
    for copy in copies:
        copy.wait_recv()

    lanes = ids.shape[-1]

    def first_id(b):
        return ((((x + b) % RING) * RING + y) * N_NEG + neg) * owned

    def tally(b):
        name = lax.broadcasted_iota(jnp.int32, (owned, lanes), 0) + first_id(b)

        def more(i, total):
            for j in range(RING * RING):
                total = total + jnp.where(name == ids[i, j // RING, j % RING], 1.0, 0.0)
            return total

        total = lax.fori_loop(0, N_NEG, more, jnp.zeros((owned, lanes), F32))
        listed = dot(total.astype(BF16), jnp.ones((lanes, lanes), BF16), NN)
        count[b] = jnp.where(listed > 0.0, jnp.log(jnp.maximum(listed, 1.0)) * LOG2E, LOW)

    tally(0)

    for i in range(N_NEG):
        for j in range(RING * RING):
            table[pl.ds(i * RING * RING + j, 1), :] = ids[i, j // RING, j % RING]
    pos = pos_in[...]
    entry = jnp.bitwise_and(pos, lanes - 1)
    lister = pos // lanes
    listing = (
        (lister // (RING * RING)) * (RING * RING)
        + jnp.bitwise_and(lister, RING - 1) * RING
        + jnp.bitwise_and(lister // RING, RING - 1)
    )
    side = lax.broadcasted_iota(jnp.int32, (lanes, block), 0)
    chosen = jnp.where(side == listing, 1.0, 0.0).astype(BF16)
    high = (table[...] // 256).astype(F32).astype(BF16)
    low = jnp.bitwise_and(table[...], 255).astype(F32).astype(BF16)
    found = dot(high, chosen, TN) * 256.0 + dot(low, chosen, TN)
    wp[0, 0:1, :] = w_in[...] * scale
    wp[0, 1:2, :] = jnp.sum(jnp.where(side == entry, found, 0.0), axis=0, keepdims=True)
    targets = [send(wp.at[0], wp.at[4 - k], y_peer[k]) for k in (1, 2, 3)]

    def raw(b, r):
        return dot(pv[b], qv[r], NT)

    def finish_logits(b, r, value):
        value = value * (scale * LOG2E) + jnp.concatenate([count[b]] * (block // lanes), axis=1)
        top = jnp.max(value, axis=0, keepdims=True)
        expo = jnp.exp2(value - top)
        place = pl.ds(pl.multiple_of(r * block, block), block)
        coarse = expo.astype(BF16)
        ev[b, 0, :, place] = coarse
        rest = expo - coarse.astype(F32)
        fine = rest.astype(BF16)
        ev[b, 1, :, place] = fine
        label = (lax.broadcasted_iota(jnp.int32, (owned, block), 0) + first_id(b)).astype(F32)
        missed = jnp.where(label == wp[r, 1:2, :], rest - fine.astype(F32), 0.0)
        r_b[b, :, place] = jnp.sum(missed, axis=0, keepdims=True)
        m_b[b, :, place] = top
        s_b[b, :, place] = jnp.sum(expo, axis=0, keepdims=True)

    def logits(b, r):
        finish_logits(b, r, raw(b, r))

    own_p.wait()
    own_q.wait()
    logits(0, 0)

    from_z, from_core = {}, {}

    def pass_on(r, sub):
        view = qv.at[r, rows(zp, core, sub)]
        from_z[r, sub] = send(view, view, z_up if sub == 0 else z_down)
        from_core[r, 0, sub] = send(view, view, other)

    def pass_over(r, sub):
        from_z[r, sub].wait_recv()
        view = qv.at[r, rows(1 - zp, core, sub)]
        from_core[r, 1, sub] = send(view, view, other)

    def have(r):
        for key in from_core:
            if key[0] == r:
                from_core[key].wait_recv()

    def to_core(b):
        for k in range(RING):
            col = pl.ds(pl.multiple_of((((z + k) % RING) * 2 + 1 - core) * strip, strip), strip)
            crossed.append(send(pv.at[b, :, col], px.at[k, b], other))

    crossed = []
    to_core(0)
    pl.loop(1, RING)(tally)
    q_right[0].wait_recv()
    q_far0 = send(qv.at[3, rows(zp, core, 0)], qv.at[2, rows(zp, core, 0)], y_peer[1])
    pass_on(3, 0)
    q_left[0].wait_recv()
    q_far1 = send(qv.at[1, rows(zp, core, 1)], qv.at[2, rows(zp, core, 1)], y_peer[3])
    pass_on(1, 1)
    p_right[0].wait_recv()
    p_far0 = send(pv.at[3, lo], pv.at[2, lo], x_peer[1])
    p_left[0].wait_recv()
    p_far1 = send(pv.at[1, hi], pv.at[2, hi], x_peer[3])
    q_right[1].wait_recv()
    pass_on(3, 1)
    q_left[1].wait_recv()
    pass_on(1, 0)
    pass_over(3, 0)
    pass_over(1, 1)
    q_far0.wait_recv()
    pass_on(2, 0)
    q_far1.wait_recv()
    pass_on(2, 1)
    pass_over(3, 1)
    pass_over(1, 0)
    have(1)
    have(3)
    for copy in targets:
        copy.wait_recv()
    pl.loop(0, 2)(lambda j: logits(0, 1 + 2 * j))
    p_right[1].wait_recv()
    p_left[1].wait_recv()
    to_core(1)
    to_core(3)

    @pl.loop(0, 6)
    def _(i):
        j = i % 3
        logits(1 + 2 * (i // 3), j + j // 2)

    pass_over(2, 0)
    pass_over(2, 1)
    have(2)
    pl.loop(0, 3)(lambda i: logits(i + i // 2, 2))
    p_far0.wait_recv()
    p_far1.wait_recv()
    to_core(2)

    def merge(pairs):
        top = pairs[0][0]
        for m, _ in pairs[1:]:
            top = jnp.maximum(top, m)
        return top, sum(mass * jnp.exp2(m - top) for m, mass in pairs)

    def within(r):
        return pl.ds(r * block, block)

    def share(r):
        top, mass = merge([(m_b[b, :, within(r)], s_b[b, :, within(r)]) for b in range(RING)])
        st_own[r, 0:1, :] = top
        st_own[r, 1:2, :] = mass
        return [send(st_own.at[r], st_in.at[k, r], n_peer[k]) for k in range(1, N_NEG)]

    def share_on(r):
        for copy in first_round[r]:
            copy.wait_recv()
        refs = [st_own.at[r]] + [st_in.at[k, r] for k in range(1, N_NEG)]
        top, mass = merge([(ref[0:1, :], ref[1:2, :]) for ref in refs])
        st_mid[r, 0:1, :] = top
        st_mid[r, 1:2, :] = mass
        return [send(st_mid.at[r], st_y.at[k, r], y_peer[k]) for k in (1, 2, 3)]

    first_round, second_round = [], []
    value = raw(2, 0)
    for r in range(1, RING):
        later = raw(2, r)
        finish_logits(2, r - 1, value)
        first_round.append(share(r - 1))
        value = later
    finish_logits(2, RING - 1, value)
    first_round.append(share(RING - 1))
    for r in range(RING):
        second_round.append(share_on(r))
    for copies in second_round:
        for copy in copies:
            copy.wait_recv()
    for r in range(RING):
        refs = [st_mid.at[r]] + [st_y.at[k, (r + k) % RING] for k in (1, 2, 3)]
        top, mass = merge([(ref[0:1, :], ref[1:2, :]) for ref in refs])
        weight = wp[r, 0:1, :] / mass
        for b in range(RING):
            factor[b, :, within(r)] = jnp.exp2(m_b[b, :, within(r)] - top) * weight

    def gradient(b):
        label = (lax.broadcasted_iota(jnp.int32, (owned, block), 0) + first_id(b)).astype(F32)
        for r in range(RING):
            place = pl.ds(r * block, block)
            taken = wp[r, 0:1, :] - r_b[b, :, place] * factor[b, :, place]
            hit = jnp.where(label == wp[r, 1:2, :], taken, 0.0)
            expo = ev[b, 0, :, place].astype(F32) + ev[b, 1, :, place].astype(F32)
            gv[b, :, place] = (expo * factor[b, :, place] - hit).astype(BF16)

    wide = width // 4

    def passage_part(b, col):
        return dot(gv[b], qv[:, :, col].reshape(RING * block, col.size), NN)

    far = {}
    gradient(2)
    for start, size in ((0, 1), (4, 1), (1, 1), (5, 1), (2, 2), (6, 2)):
        col = pl.ds(start * strip, size * strip)
        pg[1, :, col] = passage_part(2, col).astype(BF16)
        to = x_peer[1] if start < 4 else x_peer[3]
        far[start] = send(pg.at[1, :, col], pg_first.at[:, col], to)
    grads = [send(gv.at[2], gx.at[2], other)]
    for b in (1, 3, 0):
        gradient(b)
        grads.append(send(gv.at[b], gx.at[b], other))
    for copy in grads + crossed:
        copy.wait_recv()
    for copy in crossed + [p_far0, p_far1]:
        copy.wait_send()

    def query_part(r):
        @pl.loop(0, 2 * RING)
        def _(i):
            k, level = i // 2, i % 2
            place = pl.ds(pl.multiple_of(r * block + level * mid, mid), mid)
            col = pl.ds(pl.multiple_of((((z + k) % RING) * 2 + core) * strip, strip), strip)
            mine = dot(
                gv[:, :, place].reshape(RING * owned, mid),
                pv[:, :, col].reshape(RING * owned, strip),
                TN,
            )
            theirs = dot(
                gx[:, :, place].reshape(RING * owned, mid),
                px[k].reshape(RING * owned, strip),
                TN,
            )
            out = pl.ds(pl.multiple_of(k * strip, strip), strip)
            ev[r, level, :, out] = (mine + theirs).astype(BF16)

    mid = block // 2
    quarter = mid // 2

    def span(part):
        return pl.ds(0, mid) if part is None else pl.ds(part * quarter, quarter)

    def along_y(level, k):
        return lambda rel, part: ev.at[rel, level, span(part), pl.ds(k * strip, strip)]

    def along_z(r, level):
        return lambda rel, part: ev.at[r, level, span(part), pl.ds(rel * strip, strip)]

    def spare(first, k):
        col = pl.ds(pl.multiple_of((2 * k + 1 - core) * strip, strip), strip)
        return lambda way: pv.at[first + way, :, col]

    def landing(level):
        return lambda way: q_land.at[way, pl.ds(level * mid, mid)]

    a_y = [
        RingScatter(send, y_peer[1], y_peer[3], along_y(0, k), ay1.at[k], spare(0, k)) for k in range(RING)
    ]
    b_z = [RingScatter(send, z_up, z_down, along_z(r, 1), bz1.at[r], spare(2, r)) for r in range(RING)]
    a_z = RingScatter(send, z_up, z_down, along_z(0, 0), az1, landing(0))
    b_y = RingScatter(send, y_peer[1], y_peer[3], along_y(1, 0), by1, landing(1))
    order = (2, 1, 3, 0)

    def near_part(b, n):
        col = pl.ds(n * wide, wide)
        value = passage_part(b, col)
        if (b == 1) == (n < 2):
            for start in (2 * n, 2 * n + 1):
                if start in far:
                    far[start].wait_recv()
            value = value + pg_first[:, col].astype(F32)
        pg[b - 1, :, col] = value.astype(BF16)
        send(pg.at[b - 1, :, col], p_land.at[0 if b == 1 else 1, :, col], x_peer[b])

    query_part(2)
    for k in order:
        a_y[k].start()
    b_z[2].start()
    for b, n in ((1, 2), (3, 0), (1, 3), (3, 1)):
        near_part(b, n)
    b_z[2].middle()
    query_part(1)
    b_z[1].start()
    query_part(3)
    b_z[3].start()
    b_z[2].finish()
    b_y.start()
    for k in order:
        a_y[k].middle()
    b_z[1].middle()
    query_part(0)
    b_z[0].start()
    b_z[3].middle()
    for b, n in ((1, 0), (3, 2), (1, 1), (3, 3)):
        near_part(b, n)
    b_z[1].finish()
    b_z[0].middle()
    b_z[3].finish()
    b_y.middle()
    a_y[2].finish()
    a_z.start()
    for copy in far.values():
        copy.wait_send()
    for n in range(4):
        col = pl.ds(n * wide, wide)
        pg[1, :, col] = passage_part(0, col).astype(BF16)
    p_copy = pltpu.make_async_copy(pg.at[1], p_own, sems.new())
    p_copy.start()
    b_z[0].finish()
    a_y[1].finish()
    a_y[3].finish()
    a_z.middle()
    a_y[0].finish()
    upper = pltpu.make_async_copy(along_y(0, 0)(0, None), q_own.at[pl.ds(0, mid)], sems.new())
    lower = pltpu.make_async_copy(along_y(1, 0)(0, None), q_own.at[pl.ds(mid, mid)], sems.new())
    upper.start()
    lower.start()
    for copy in sent:
        copy.wait()
    p_copy.wait()
    upper.wait()
    lower.wait()


def add_up(q_own, q_land, p_own, p_land, q_out, p_out):
    q_out[...] = (q_own[...].astype(F32) + q_land[0].astype(F32) + q_land[1].astype(F32)).astype(BF16)
    p_out[...] = p_own[...].astype(F32) + p_land[0].astype(F32) + p_land[1].astype(F32)


def body(queries, passages, list_owner, list_row, positive, row_weight):
    block, width = queries.shape
    owned = passages.shape[0]
    lanes = list_row.shape[1]
    strip = width // N_NEG
    mid = block // 2
    any_space = pl.BlockSpec(memory_space=pl.ANY)
    vmem = pl.BlockSpec(memory_space=pltpu.VMEM)
    wide = width // 4
    scratch = [
        pltpu.VMEM((RING, block, width), BF16),
        pltpu.VMEM((RING, owned, width), BF16),
        pltpu.VMEM((RING, RING, owned, strip), BF16),
        pltpu.VMEM((RING, 2, owned, RING * block), BF16),
        pltpu.VMEM((RING, owned, RING * block), BF16),
        pltpu.VMEM((RING, owned, RING * block), BF16),
        pltpu.VMEM((3, owned, width), BF16),
        pltpu.VMEM((owned, width), BF16),
        pltpu.VMEM((RING, 2, mid // 2, strip), BF16),
        pltpu.VMEM((2, mid // 2, strip), BF16),
        pltpu.VMEM((RING, 2, mid // 2, strip), BF16),
        pltpu.VMEM((2, mid // 2, strip), BF16),
        pltpu.VMEM((N_NEG, RING, RING, 1, lanes), jnp.int32),
        pltpu.VMEM((lanes, lanes), jnp.int32),
        pltpu.VMEM((RING, owned, lanes), F32),
        pltpu.VMEM((RING, 2, block), F32),
        pltpu.VMEM((RING, 1, RING * block), F32),
        pltpu.VMEM((RING, 1, RING * block), F32),
        pltpu.VMEM((RING, 1, RING * block), F32),
        pltpu.VMEM((RING, 2, block), F32),
        pltpu.VMEM((N_NEG, RING, 2, block), F32),
        pltpu.VMEM((RING, 2, block), F32),
        pltpu.VMEM((RING, RING, 2, block), F32),
        pltpu.VMEM((RING, 1, RING * block), F32),
        pltpu.SemaphoreType.DMA((SEMS,)),
    ]
    flops = 6 * RING * block * RING * owned * width
    q_own, q_land, p_own, p_land = pl.pallas_call(
        kernel,
        out_shape=(
            jax.ShapeDtypeStruct((block, strip), BF16),
            jax.ShapeDtypeStruct((2, block, strip), BF16),
            jax.ShapeDtypeStruct((owned, width), BF16),
            jax.ShapeDtypeStruct((2, owned, width), BF16),
        ),
        in_specs=[any_space, any_space, vmem, vmem, vmem, vmem],
        out_specs=(any_space,) * 4,
        scratch_shapes=scratch,
        compiler_params=pltpu.CompilerParams(
            collective_id=0, has_side_effects=True, vmem_limit_bytes=62 * 2**20
        ),
        cost_estimate=pl.CostEstimate(flops=flops, bytes_accessed=40 * 2**20, transcendentals=0),
        name="contrastive",
    )(
        queries,
        passages,
        list_owner.reshape(1, lanes),
        list_row,
        positive.reshape(1, block),
        row_weight.reshape(1, block),
    )
    steps = 2
    q_rows, p_rows = block // steps, owned // steps
    return pl.pallas_call(
        add_up,
        grid=(steps,),
        out_shape=(
            jax.ShapeDtypeStruct((block, strip), BF16),
            jax.ShapeDtypeStruct((owned, width), F32),
        ),
        in_specs=[
            pl.BlockSpec((q_rows, strip), lambda i: (i, 0)),
            pl.BlockSpec((2, q_rows, strip), lambda i: (0, i, 0)),
            pl.BlockSpec((p_rows, width), lambda i: (i, 0)),
            pl.BlockSpec((2, p_rows, width), lambda i: (0, i, 0)),
        ],
        out_specs=(
            pl.BlockSpec((q_rows, strip), lambda i: (i, 0)),
            pl.BlockSpec((p_rows, width), lambda i: (i, 0)),
        ),
        compiler_params=pltpu.CompilerParams(vmem_limit_bytes=60 * 2**20),
        name="add_up",
    )(q_own, q_land, p_own, p_land)


def solution(mesh):
    in_specs = (
        P("dp", None),
        P(("dp", "neg"), None),
        P("neg", "dp", None),
        P("neg", "dp"),
        P("dp"),
        P("dp"),
    )
    out_specs = (P("dp", "neg"), P(("dp", "neg"), None))
    return jax.shard_map(body, mesh=mesh, in_specs=in_specs, out_specs=out_specs, check_vma=False)
```
